32 devices in a mesh: grid: 8 (over z, y), member: 4 (over x, core).
Axes of the slice: x: 2, y: 2, z: 4, core: 2. Of those that a mesh axis runs over, the one named last changes fastest.
Arguments:
- latent: bfloat16 [8, 2560, 1024], P('member', 'grid'), may hold values from -6 to 6
- grid_feat: bfloat16 [1024, 1024], P('grid'), may hold values from -6 to 6
- w_query: bfloat16 [1024, 1024], replicated, may hold values from -0.1875 to 0.1875
- w_key: bfloat16 [1024, 1024], replicated, may hold values from -0.1875 to 0.1875
- w_value: bfloat16 [1024, 1024], replicated, may hold values from -0.1875 to 0.1875
- w_out: bfloat16 [96, 1024], replicated, may hold values from -0.1875 to 0.1875
- truth: float32 [96, 1024], P(None, 'grid'), may hold values from -6 to 6
- area: float32 [1024], P('grid'), may hold values from 1 to 10
- var_weight: float32 [96], replicated, may hold values from 1 to 10
- send_rows: int32 [8, 8, 24], P('grid'), may hold values from 0 to 319, as said below
- neighbours: int32 [1024, 16], P('grid'), may hold values from 0 to 191, as said below
- live_count: int32 [1024], P('grid'), may hold values from 8 to 16
Outputs:
- latent_grad: float32 [8, 2560, 1024], P('member', 'grid')
The draws below stay inside these ranges and needn't reach their ends.
Inputs may be any that keep to these rules, and one draw needn't show every extreme that they name: send_rows[s, d, c] is the row, local to owner s, that owner s sends to grid device d in place c; the 24 entries of one s and d are distinct. neighbours[g, k] = s * 24 + c names place c of what owner s sends to the grid device of point g; every place named is one that some point of that device uses, and on some device every place of every owner is used; slots k >= live_count[g] are ignored.
All inputs are finite; a program needn't handle non-finite values.
Results may differ from the reference program's by a relative error of at most 0.0078.
Values may be sent and summed in bfloat16 or wider, within the bound.
No kernel may reach another device: no remote copies, remote signals or barrier semaphores. Data moves between devices by JAX's collectives and lax.ppermute only.
A program may use at most 128 MiB of HBM per device.

```python
import math
import jax
import jax.numpy as jnp
from jax import lax

D = 1024
H = 16
DH = 64
VARS = 96
SLOTS = 16
CAP = 24
G_DEV = 128
MESH_DEV = 320
GRID = 1024
MESH = 2560
MEMBERS = 8
N_GRID = 8


def link_counts(key):
    base_key = jax.random.fold_in(key, 11)
    first_key, second_key = jax.random.split(base_key)
    heavy = jax.random.randint(first_key, (), 0, N_GRID)
    light = jax.random.randint(second_key, (N_GRID, N_GRID), 2, CAP // 2 + 1)
    column = jnp.arange(N_GRID)[None, :]
    return jnp.where(column == heavy, CAP, light).astype(jnp.int32)


def draw_send_rows(key, part):
    keys = jax.random.split(jax.random.fold_in(key, 5), N_GRID * N_GRID)

    def pick_rows(one_key):
        return jax.random.permutation(one_key, MESH_DEV)[:CAP].astype(jnp.int32)
    return jax.vmap(pick_rows)(keys).reshape(N_GRID, N_GRID, CAP)


def draw_neighbours(key, part):
    counts = link_counts(key)
    keys = jax.random.split(jax.random.fold_in(key, 17), N_GRID)
    slot_source = jnp.arange(N_GRID * CAP) // CAP
    slot_place = jnp.arange(N_GRID * CAP) % CAP

    def one_device(target, device_key):
        live = slot_place < counts[slot_source, target]
        order = jnp.argsort(1 - live.astype(jnp.int32), stable=True).astype(jnp.int32)
        total = jnp.sum(live.astype(jnp.int32))
        first_key, second_key = jax.random.split(device_key)
        spread = jnp.arange(G_DEV * 8, dtype=jnp.int32) % total
        spread = jax.random.permutation(first_key, spread).reshape(G_DEV, 8)
        extra = jax.random.randint(second_key, (G_DEV, SLOTS - 8), 0, total)
        picks = jnp.concatenate([spread, extra.astype(jnp.int32)], axis=1)
        return order[picks]
    result = jax.vmap(one_device)(jnp.arange(N_GRID), keys)
    return result.reshape(N_GRID * G_DEV, SLOTS).astype(jnp.int32)


def with_ends(drawn, key, smallest, high):
    longest = drawn.shape.index(max(drawn.shape))
    spots = []
    for shift in (0, 1):
        where = [jax.random.randint(jax.random.fold_in(key, axis), (), 0, length) for axis, length in enumerate(drawn.shape)]
        where[longest] = (where[longest] + shift) % drawn.shape[longest]
        spots.append(tuple(where))
    return drawn.at[spots[0]].set(smallest).at[spots[1]].set(high)


def levels(stream_key, dims, pieces, smallest, high):
    factor_of = 1.0
    for position, parts in pieces:
        heights = jax.random.uniform(jax.random.fold_in(jax.random.fold_in(stream_key, 6), position), (parts,), jnp.float32, smallest / len(pieces), high / len(pieces))
        factor_of = factor_of * jnp.repeat(jnp.exp(heights), dims[position] // parts).reshape((-1,) + (1,) * (len(dims) - 1 - position))
    return factor_of


def scatter_about(own_key, extent, scale, limit, cuts=(), kind=jnp.bfloat16):
    array = scale * jax.random.normal(own_key, extent, jnp.float32)
    if cuts:
        array = array * levels(own_key, extent, cuts, -0.22, 0.18)
    return jnp.clip(array, -limit, limit).astype(kind)


def setup_inputs(seed: int = 0) -> dict:
    key_of = jax.random.split(jax.random.key(seed), 13)
    latent = scatter_about(key_of[0], (MEMBERS, MESH, D), 1.0, 6.0, ((0, 4), (1, 8)))
    grid_feat = scatter_about(key_of[1], (GRID, D), 1.0, 6.0, ((0, 8),))
    w_query = scatter_about(key_of[2], (D, D), D ** -0.5, 0.1875)
    w_key = scatter_about(key_of[3], (D, D), D ** -0.5, 0.1875)
    w_value = scatter_about(key_of[4], (D, D), D ** -0.5, 0.1875)
    w_out = scatter_about(key_of[5], (VARS, D), D ** -0.5, 0.1875)
    truth = scatter_about(key_of[6], (VARS, GRID), 1.0, 6.0, ((1, 8),), jnp.float32)
    area = jnp.clip(jnp.exp(math.log(10.0) - 2.3025851 * jax.random.uniform(key_of[7], (GRID,), jnp.float32) ** levels(key_of[7], (GRID,), ((0, 8),), -0.2, 0.2)), 1.0, 10.0)
    var_weight = jnp.clip(jnp.exp(jax.random.uniform(key_of[8], (VARS,), jnp.float32, math.log(1.0), math.log(10.0))), 1.0, 10.0)
    send_rows = draw_send_rows(jax.random.fold_in(key_of[12], 71), 0)
    neighbours = draw_neighbours(jax.random.fold_in(key_of[12], 71), 0)
    live_count = with_ends(jax.random.randint(key_of[11], (GRID,), 8, SLOTS + 1), jax.random.fold_in(key_of[11], 1), 8, SLOTS).astype(jnp.int32)
    return {"latent": latent, "grid_feat": grid_feat, "w_query": w_query, "w_key": w_key, "w_value": w_value, "w_out": w_out, "truth": truth, "area": area, "var_weight": var_weight, "send_rows": send_rows, "neighbours": neighbours, "live_count": live_count}


def rounded(value):
    return lax.optimization_barrier(value.astype(jnp.bfloat16))

def ensemble_gradient(everyone, mine, truth, area, var_weight):
    total = everyone.shape[0]
    miss = mine - truth[None]
    first = miss / jnp.sqrt(1.0 + miss * miss) / total
    paired = mine[:, None] - everyone[None]
    second = lax.optimization_barrier(jnp.sum(paired / jnp.sqrt(1.0 + paired * paired), axis=1)) / (total * (total - 1))
    return area[None, None, :] * var_weight[None, :, None] * (first - second)

def attend(query_blk, keys_blk, values_blk, live_blk):
    scale = DH ** (-0.5)
    scores = jnp.einsum('ghd,gshd->ghs', query_blk.astype(jnp.float32), keys_blk.astype(jnp.float32)) * scale
    live = jnp.arange(SLOTS)[None, None, :] < live_blk[:, None, None]
    raised = jnp.where(live, jnp.exp(scores), jnp.float32(0.0))
    probs = rounded(raised / lax.optimization_barrier(jnp.sum(raised, axis=2, keepdims=True)))
    attended = rounded(jnp.einsum('ghs,gshd->ghd', probs.astype(jnp.float32), values_blk.astype(jnp.float32)))
    return (probs, attended)

def reference(latent, grid_feat, w_query, w_key, w_value, w_out, truth, area, var_weight, send_rows, neighbours, live_count):
    f32 = jnp.float32
    query = rounded(jnp.dot(grid_feat, w_query, preferred_element_type=f32))
    query_blocks = query.reshape(N_GRID, G_DEV, H, DH)
    nbr_blocks = neighbours.reshape(N_GRID, G_DEV, SLOTS)
    live_blocks = live_count.reshape(N_GRID, G_DEV)
    source = (nbr_blocks // CAP).astype(jnp.int32)
    place = (nbr_blocks % CAP).astype(jnp.int32)
    device_index = jnp.arange(N_GRID, dtype=jnp.int32)[:, None, None]
    mesh_row = (source * MESH_DEV + send_rows[source, device_index, place]).astype(jnp.int32)
    out_wide = w_out.astype(f32)
    keys_all, values_all, preds = ([], [], [])
    for member in range(MEMBERS):
        keys_mesh = rounded(jnp.dot(latent[member], w_key, preferred_element_type=f32))
        values_mesh = rounded(jnp.dot(latent[member], w_value, preferred_element_type=f32))
        keys_all.append(keys_mesh)
        values_all.append(values_mesh)

        def forward_block(items, keys_mesh=keys_mesh, values_mesh=values_mesh):
            query_blk, rows_blk, live_blk = items
            keys_blk = keys_mesh[rows_blk.reshape(-1)].reshape(G_DEV, SLOTS, H, DH)
            values_blk = values_mesh[rows_blk.reshape(-1)].reshape(G_DEV, SLOTS, H, DH)
            probs, attended = attend(query_blk, keys_blk, values_blk, live_blk)
            return jnp.einsum('vd,gd->vg', out_wide, attended.reshape(G_DEV, D).astype(f32))
        blocks = lax.map(forward_block, (query_blocks, mesh_row, live_blocks))
        preds.append(jnp.transpose(blocks, (1, 0, 2)).reshape(VARS, GRID))
    predicted = jnp.stack(preds)

    def member_grad(mine):
        return ensemble_gradient(predicted, mine[None], truth, area, var_weight)[0]
    dpred = rounded(lax.map(member_grad, predicted))
    key_wide = w_key.astype(f32)
    value_wide = w_value.astype(f32)
    results = []
    for member in range(MEMBERS):
        keys_mesh = keys_all[member]
        values_mesh = values_all[member]
        dpred_blocks = jnp.transpose(dpred[member].reshape(VARS, N_GRID, G_DEV), (1, 0, 2))

        def backward_block(carry, items, keys_mesh=keys_mesh, values_mesh=values_mesh):
            key_sum, value_sum = carry
            query_blk, rows_blk, live_blk, dpred_blk = items
            flat_rows = rows_blk.reshape(-1)
            keys_blk = keys_mesh[flat_rows].reshape(G_DEV, SLOTS, H, DH)
            values_blk = values_mesh[flat_rows].reshape(G_DEV, SLOTS, H, DH)
            probs, attended = attend(query_blk, keys_blk, values_blk, live_blk)
            d_attended = rounded(jnp.einsum('vg,vd->gd', dpred_blk.astype(f32), out_wide)).reshape(G_DEV, H, DH)
            d_wide = d_attended.astype(f32)
            d_probs = jnp.einsum('ghd,gshd->ghs', d_wide, values_blk.astype(f32))
            probs_wide = probs.astype(f32)
            d_scores = probs_wide * (d_probs - lax.optimization_barrier(jnp.sum(probs_wide * d_probs, axis=2, keepdims=True))) * DH ** (-0.5)
            d_keys = jnp.einsum('ghs,ghd->gshd', d_scores, query_blk.astype(f32)).reshape(G_DEV * SLOTS, D)
            d_values = jnp.einsum('ghs,ghd->gshd', probs_wide, d_wide).reshape(G_DEV * SLOTS, D)
            key_sum = key_sum + jax.ops.segment_sum(d_keys, flat_rows, num_segments=MESH)
            value_sum = value_sum + jax.ops.segment_sum(d_values, flat_rows, num_segments=MESH)
            return ((key_sum, value_sum), None)
        start = (jnp.zeros((MESH, D), f32), jnp.zeros((MESH, D), f32))
        (key_sum, value_sum), unused = lax.scan(backward_block, start, (query_blocks, mesh_row, live_blocks, dpred_blocks))
        grad = jnp.dot(key_sum, key_wide.T, precision=lax.Precision.HIGHEST) + jnp.dot(value_sum, value_wide.T, precision=lax.Precision.HIGHEST)
        results.append(grad)
    return jnp.stack(results)
```

```python
import functools

import jax
import jax.numpy as jnp
from jax import lax
from jax.experimental import pallas as pl
from jax.experimental.pallas import tpu as pltpu
from jax.sharding import PartitionSpec as P

H = 16
LANES = 128
F32 = jnp.float32
BF16 = jnp.bfloat16
NN = (((1,), (0,)), ((), ()))
NT = (((1,), (1,)), ((), ()))
TN = (((0,), (0,)), ((), ()))
VMEM = pl.BlockSpec(memory_space=pltpu.VMEM)


def dot(a, b, dims=NN):
    return lax.dot_general(a, b, dims, preferred_element_type=F32)


def call(kernel, out_shape, operands, scratch=(), flops=0, limit=40):
    single = not isinstance(out_shape, (list, tuple))
    bytes_accessed = sum(x.size * x.dtype.itemsize for x in operands)
    return pl.pallas_call(
        kernel,
        out_shape=out_shape,
        in_specs=[VMEM] * len(operands),
        out_specs=VMEM if single else [VMEM] * len(out_shape),
        scratch_shapes=list(scratch),
        compiler_params=pltpu.CompilerParams(vmem_limit_bytes=limit * 1024 * 1024),
        cost_estimate=pl.CostEstimate(
            flops=flops, bytes_accessed=bytes_accessed, transcendentals=0
        ),
    )(*operands)


def of_member(block, member, members, chunks, capacity):
    step = members * capacity
    first = member * capacity
    return jnp.concatenate(
        [block[c * step + first : c * step + first + capacity] for c in range(chunks)], axis=0
    )


def by_chunk(blocks, chunks, capacity):
    return jnp.concatenate(
        [b[c * capacity : (c + 1) * capacity] for c in range(chunks) for b in blocks], axis=0
    )


def gather_kernel(members, chunks, capacity, latent_ref, rows_ref, *out_refs):
    own_rows = latent_ref.shape[1]
    total = chunks * capacity
    ids = lax.broadcasted_iota(jnp.int32, (total, own_rows), 1)
    pick = (rows_ref[...] == ids).astype(F32).astype(BF16)
    picked = [dot(pick, latent_ref[m]) for m in range(members)]
    step = members * capacity
    rows = by_chunk(picked, chunks, capacity).astype(BF16)
    for c in range(chunks):
        out_refs[c][...] = rows[c * step : (c + 1) * step]


def query_kernel(head_size, feat_ref, w_ref, out_ref):
    points, width = feat_ref.shape
    per = LANES // head_size
    query = dot(feat_ref[...], w_ref[...]).astype(BF16)
    head = lax.broadcasted_iota(jnp.int32, (points, width), 1) // head_size % per
    for p in range(per):
        out_ref[p * points : (p + 1) * points, :] = jnp.where(
            head == p, query, jnp.zeros_like(query)
        )


def forward_kernel(
    members, chunks, capacity, head_size, qm_ref, wk_ref, wv_ref, wout_ref, mult_ref, *refs
):
    chunk_refs = refs[:chunks]
    pred_ref, weight_ref, v_ref, rows_scr, k_scr = refs[chunks:]
    width = wk_ref.shape[0]
    points = mult_ref.shape[1]
    per = LANES // head_size
    groups = width // LANES
    scale = head_size ** (-0.5)
    step = members * capacity
    for c in range(chunks):
        rows_scr[c * step : (c + 1) * step, :] = chunk_refs[c][...]
    tile = 2 * LANES

    @pl.loop(0, width // tile)
    def project(t):
        cols = pl.ds(pl.multiple_of(t * tile, tile), tile)
        keys = dot(rows_scr[...], wk_ref[:, cols])
        values = dot(rows_scr[...], wv_ref[:, cols])
        for m in range(members):
            k_scr[m, :, cols] = of_member(keys, m, members, chunks, capacity).astype(BF16)
            v_ref[m, :, cols] = of_member(values, m, members, chunks, capacity).astype(BF16)

    mult = jnp.concatenate([mult_ref[...]] * per, axis=1)
    named = mult > 0.0
    head = lax.broadcasted_iota(jnp.int32, (points, LANES), 1) // head_size
    for m in range(members):
        pred = jnp.zeros(pred_ref.shape[1:], F32)
        for j in range(groups):
            cols = slice(j * LANES, (j + 1) * LANES)
            scores = dot(k_scr[m, :, cols], qm_ref[:, cols], NT) * scale
            raised = jnp.where(named, jnp.exp(scores), 0.0)
            denom = jnp.sum(mult * raised, axis=0, keepdims=True)
            probs = (raised * (1.0 / denom)).astype(BF16)
            weights = (mult * probs.astype(F32)).astype(BF16)
            weight_ref[m, j] = weights
            both = dot(weights, v_ref[m, :, cols], TN)
            attended = both[:points]
            for p in range(1, per):
                attended = jnp.where(head == p, both[p * points : (p + 1) * points], attended)
            pred = pred + dot(wout_ref[:, cols], attended.astype(BF16), NT)
        pred_ref[m] = pred


def backward_kernel(
    members,
    chunks,
    capacity,
    head_size,
    qm_ref,
    wk_ref,
    wv_ref,
    wout_ref,
    every_ref,
    mine_ref,
    truth_ref,
    area_ref,
    var_ref,
    weight_ref,
    v_ref,
    *refs,
):
    out_refs = refs[:chunks]
    da_scr, dk_scr, dv_scr = refs[chunks:]
    width = wk_ref.shape[0]
    points = truth_ref.shape[1]
    total = every_ref.shape[0]
    per = LANES // head_size
    groups = width // LANES
    scale = head_size ** (-0.5)
    step = members * capacity
    factor = area_ref[...] * var_ref[...]
    head = lax.broadcasted_iota(jnp.int32, (points, width), 1) // head_size % per
    for m in range(members):
        mine = mine_ref[m]
        miss = mine - truth_ref[...]
        first = miss / jnp.sqrt(1.0 + miss * miss) / total
        second = jnp.zeros_like(mine)
        for f in range(total):
            paired = mine - every_ref[f]
            second = second + paired / jnp.sqrt(1.0 + paired * paired)
        dpred = (factor * (first - second / (total * (total - 1)))).astype(BF16)
        d_attended = dot(dpred, wout_ref[...], TN).astype(BF16)
        for p in range(per):
            da_scr[m, p * points : (p + 1) * points, :] = jnp.where(
                head == p, d_attended, jnp.zeros_like(d_attended)
            )
    for j in range(groups):
        cols = slice(j * LANES, (j + 1) * LANES)
        d_keys, d_values = [], []
        for m in range(members):
            d_probs = dot(v_ref[m, :, cols], da_scr[m, :, cols], NT)
            weights = weight_ref[m, j].astype(F32)
            inner = jnp.sum(weights * d_probs, axis=0, keepdims=True)
            d_scores = (weights * (d_probs - inner) * scale).astype(BF16)
            d_keys.append(dot(d_scores, qm_ref[:, cols]))
            d_values.append(dot(weight_ref[m, j], da_scr[m, :, cols]))
        dk_scr[:, cols] = by_chunk(d_keys, chunks, capacity).astype(BF16)
        dv_scr[:, cols] = by_chunk(d_values, chunks, capacity).astype(BF16)
    tile = 2 * LANES

    @pl.loop(0, width // tile)
    def project(t):
        cols = pl.ds(pl.multiple_of(t * tile, tile), tile)
        rows = dot(dk_scr[...], wk_ref[cols, :], NT) + dot(dv_scr[...], wv_ref[cols, :], NT)
        rows = rows.astype(BF16)
        for c in range(chunks):
            out_refs[c][:, cols] = rows[c * step : (c + 1) * step]


def scatter_kernel(members, chunks, capacity, rows_ref, *refs):
    chunk_refs = refs[:chunks]
    out_ref = refs[chunks]
    own_rows = out_ref.shape[1]
    total = chunks * capacity
    ids = lax.broadcasted_iota(jnp.int32, (own_rows, total), 0)
    place = (rows_ref[...] == ids).astype(F32).astype(BF16)
    back = jnp.concatenate([r[...] for r in chunk_refs], axis=0).astype(F32)
    for m in range(members):
        mine = of_member(back, m, members, chunks, capacity).astype(BF16)
        out_ref[m] = dot(place, mine)


def on_device(
    chunks,
    latent,
    grid_feat,
    w_query,
    w_key,
    w_value,
    w_out,
    truth,
    area,
    var_weight,
    send_rows,
    neighbours,
    live_count,
):
    members, own_rows, width = latent.shape
    points, slots = neighbours.shape
    variables = w_out.shape[0]
    capacity = send_rows.shape[2]
    head_size = width // H
    per = LANES // head_size
    groups = width // LANES
    step = members * capacity
    received = chunks * capacity
    me = lax.axis_index("grid")
    shifts = jnp.arange(chunks, dtype=jnp.int32)
    targets = lax.rem(me + shifts, chunks)
    sources = lax.rem(me + chunks - shifts, chunks)

    def sent(blocks, sign):
        pairs = lambda s: [(i, (i + sign * s) % chunks) for i in range(chunks)]
        return [blocks[0]] + [
            lax.ppermute(blocks[s], "grid", pairs(s)) for s in range(1, chunks)
        ]

    rows_out = send_rows[0][targets].reshape(-1)
    chunk_shape = jax.ShapeDtypeStruct((step, width), BF16)
    outgoing = call(
        functools.partial(gather_kernel, members, chunks, capacity),
        [chunk_shape] * chunks,
        [latent, rows_out[:, None]],
        flops=2 * members * received * own_rows * width,
    )
    arrived = sent(outgoing, 1)
    query = call(
        functools.partial(query_kernel, head_size),
        jax.ShapeDtypeStruct((per * points, width), BF16),
        [grid_feat, w_query],
        flops=2 * points * width * width,
    )
    row_ids = (sources[:, None] * capacity + jnp.arange(capacity, dtype=jnp.int32)).reshape(-1)
    live = jnp.arange(slots)[:, None] < live_count[None, :]
    names = jnp.where(live, neighbours.T, -1)
    mult = jnp.sum((row_ids[None, :, None] == names[:, None, :]).astype(F32), axis=0)

    predicted, weights, values = call(
        functools.partial(forward_kernel, members, chunks, capacity, head_size),
        [
            jax.ShapeDtypeStruct((members, variables, points), F32),
            jax.ShapeDtypeStruct((members, groups, received, per * points), BF16),
            jax.ShapeDtypeStruct((members, received, width), BF16),
        ],
        [query, w_key, w_value, w_out, mult, *arrived],
        scratch=[
            pltpu.VMEM((chunks * step, width), BF16),
            pltpu.VMEM((members, received, width), BF16),
        ],
        flops=4 * members * received * width * width,
    )
    everyone = lax.all_gather(predicted, "member", axis=0, tiled=True)
    leaving = call(
        functools.partial(backward_kernel, members, chunks, capacity, head_size),
        [chunk_shape] * chunks,
        [
            query,
            w_key,
            w_value,
            w_out,
            everyone,
            predicted,
            truth,
            area[None, :],
            var_weight[:, None],
            weights,
            values,
        ],
        scratch=[
            pltpu.VMEM((members, per * points, width), BF16),
            pltpu.VMEM((chunks * step, width), BF16),
            pltpu.VMEM((chunks * step, width), BF16),
        ],
        flops=4 * members * received * width * width,
    )
    returned = sent(leaving, -1)
    return call(
        functools.partial(scatter_kernel, members, chunks, capacity),
        jax.ShapeDtypeStruct((members, own_rows, width), F32),
        [rows_out[None, :], *returned],
        flops=2 * members * received * own_rows * width,
    )


def solution(mesh):
    return jax.shard_map(
        functools.partial(on_device, mesh.shape["grid"]),
        mesh=mesh,
        in_specs=(
            P("member", "grid", None),
            P("grid", None),
            P(),
            P(),
            P(),
            P(),
            P(None, "grid"),
            P("grid"),
            P(),
            P("grid", None, None),
            P("grid", None),
            P("grid"),
        ),
        out_specs=P("member", "grid", None),
        check_vma=False,
    )
```

```python
import functools
import math

import jax
import jax.numpy as jnp
from jax import lax
from jax.experimental import pallas as pl
from jax.experimental.pallas import tpu as pltpu
from jax.sharding import PartitionSpec as P

H = 16
LANES = 128
ROOM = 4 * 1024 * 1024
F32 = jnp.float32
BF16 = jnp.bfloat16
NN = (((1,), (0,)), ((), ()))
NT = (((1,), (1,)), ((), ()))
TN = (((0,), (0,)), ((), ()))
VMEM = pl.BlockSpec(memory_space=pltpu.VMEM)
SMEM = pl.BlockSpec(memory_space=pltpu.SMEM)


def dot(a, b, dims=NN):
    return lax.dot_general(a, b, dims, preferred_element_type=F32)


def call(kernel, out_shape, operands, scratch=(), flops=0, scalars=(), limit=None):
    single = not isinstance(out_shape, (list, tuple))
    outs = [out_shape] if single else out_shape
    moved = sum(x.size * x.dtype.itemsize for x in [*operands, *outs])
    held = sum(math.prod(s.shape) * jnp.dtype(s.dtype).itemsize for s in scratch)
    return pl.pallas_call(
        kernel,
        out_shape=out_shape,
        in_specs=[SMEM if i in scalars else VMEM for i in range(len(operands))],
        out_specs=VMEM if single else [VMEM] * len(outs),
        scratch_shapes=list(scratch),
        compiler_params=pltpu.CompilerParams(vmem_limit_bytes=limit or moved + 2 * held + ROOM),
        cost_estimate=pl.CostEstimate(flops=flops, bytes_accessed=moved, transcendentals=0),
    )(*operands)


def of_member(block, member, members, chunks, capacity):
    step = members * capacity
    first = member * capacity
    return jnp.concatenate(
        [block[c * step + first : c * step + first + capacity] for c in range(chunks)], axis=0
    )


def by_chunk(blocks, chunks, capacity):
    return jnp.concatenate(
        [b[c * capacity : (c + 1) * capacity] for c in chunks for b in blocks], axis=0
    )


def named_rows(send_ref, me_ref, order):
    return jnp.concatenate(
        [send_ref[0, pl.ds(me_ref[0] ^ mask, 1), :] for mask in order], axis=1
    )


def one_hot(send_ref, me_ref, order, own_rows):
    rows = named_rows(send_ref, me_ref, order)
    ids = lax.broadcasted_iota(jnp.int32, (own_rows, rows.shape[1]), 0)
    return (rows == ids).astype(F32).astype(BF16)


def gather_kernel(members, order, capacity, latent_ref, send_ref, me_ref, *out_refs):
    chunks = len(order)
    pick = one_hot(send_ref, me_ref, order, latent_ref.shape[1])
    picked = [dot(pick, latent_ref[m], TN) for m in range(members)]
    step = members * capacity
    rows = by_chunk(picked, range(chunks), capacity).astype(BF16)
    for c in range(chunks):
        out_refs[c][...] = rows[c * step : (c + 1) * step]


def query_kernel(head_size, feat_ref, w_ref, out_ref):
    points, width = feat_ref.shape
    per = LANES // head_size
    query = dot(feat_ref[...], w_ref[...]).astype(BF16)
    head = lax.broadcasted_iota(jnp.int32, (points, width), 1) // head_size % per
    for p in range(per):
        out_ref[p * points : (p + 1) * points, :] = jnp.where(
            head == p, query, jnp.zeros_like(query)
        )


def project(rows, wk_ref, wv_ref, k_scr, v_ref, offset, members, chunks, capacity):
    width = wk_ref.shape[0]
    tile = 2 * LANES
    rows_here = pl.ds(offset, chunks * capacity)
    for t in range(width // tile):
        cols = slice(t * tile, (t + 1) * tile)
        keys = dot(rows, wk_ref[:, cols])
        values = dot(rows, wv_ref[:, cols])
        for m in range(members):
            k_scr[m, :, cols] = of_member(keys, m, members, chunks, capacity).astype(BF16)
            v_ref[m, rows_here, cols] = of_member(values, m, members, chunks, capacity).astype(
                BF16
            )


def raised_scores(k_scr, qm_ref, m, j, factor, bias):
    cols = slice(j * LANES, (j + 1) * LANES)
    return jnp.exp2(dot(k_scr[m, :, cols], qm_ref[:, cols], NT) * factor + bias)


def exponent(head_size):
    return head_size ** (-0.5) * math.log2(math.e)


def near_kernel(members, chunks, capacity, head_size, qm_ref, wk_ref, wv_ref, mult_ref, *refs):
    raised_ref, v_ref, k_scr = refs[chunks:]
    groups = wk_ref.shape[0] // LANES
    rows = jnp.concatenate([r[...] for r in refs[:chunks]], axis=0)
    project(rows, wk_ref, wv_ref, k_scr, v_ref, 0, members, chunks, capacity)
    mult = jnp.concatenate([mult_ref[...]] * (LANES // head_size), axis=1)
    bias = jnp.where(mult > 0.0, 0.0, -jnp.inf)
    for m in range(members):
        for j in range(groups):
            raised_ref[m, j] = raised_scores(k_scr, qm_ref, m, j, exponent(head_size), bias)


def forward_kernel(
    members,
    chunks,
    capacity,
    head_size,
    qm_ref,
    wk_ref,
    wv_ref,
    wout_ref,
    mult_ref,
    raised_ref,
    v_near_ref,
    *refs,
):
    pred_ref, weight_ref, v_ref, k_scr, att_scr = refs[chunks:]
    points = mult_ref.shape[1]
    per = LANES // head_size
    groups = wk_ref.shape[0] // LANES
    done = v_near_ref.shape[1]
    rows = jnp.concatenate([r[...] for r in refs[:chunks]], axis=0)
    v_ref[:, :done, :] = v_near_ref[...]
    project(rows, wk_ref, wv_ref, k_scr, v_ref, done, members, chunks, capacity)
    mult = jnp.concatenate([mult_ref[...]] * per, axis=1)
    bias = jnp.where(mult[done:] > 0.0, 0.0, -jnp.inf)
    steps = [(m, j) for m in range(members) for j in range(groups)]
    ahead = raised_scores(k_scr, qm_ref, *steps[0], exponent(head_size), bias)
    for i, (m, j) in enumerate(steps):
        raised = jnp.concatenate([raised_ref[m, j], ahead], axis=0)
        if i + 1 < len(steps):
            ahead = raised_scores(k_scr, qm_ref, *steps[i + 1], exponent(head_size), bias)
        root = lax.rsqrt(jnp.sum(mult * raised, axis=0, keepdims=True))
        weights = (raised * root * root * mult).astype(BF16)
        weight_ref[m, j] = weights
        both = dot(v_ref[m, :, j * LANES : (j + 1) * LANES], weights, TN)
        for p in range(per):
            first = p * head_size
            att_scr[pl.ds(j * LANES + first, head_size), :] = both[
                first : first + head_size, p * points : (p + 1) * points
            ].astype(BF16)
        if j == groups - 1:
            pred_ref[m] = dot(wout_ref[...], att_scr[...])


def return_rows(dk, dv, wk_ref, wv_ref, out_refs):
    width = wk_ref.shape[0]
    tile = 2 * LANES
    step = out_refs[0].shape[0]
    for t in range(width // tile):
        cols = slice(t * tile, (t + 1) * tile)
        rows = dot(dk, wk_ref[cols, :], NT) + dot(dv, wv_ref[cols, :], NT)
        rows = rows.astype(BF16)
        for c, out_ref in enumerate(out_refs):
            out_ref[:, cols] = rows[c * step : (c + 1) * step]


def backward_kernel(
    members,
    early,
    late,
    capacity,
    head_size,
    qm_ref,
    wk_ref,
    wv_ref,
    wout_ref,
    every_ref,
    mine_ref,
    truth_ref,
    area_ref,
    var_ref,
    weight_ref,
    v_ref,
    *refs,
):
    out_refs = refs[: len(early)]
    dk_ref, dv_ref, da_scr, dk_scr, dv_scr = refs[len(early) :]
    width = wk_ref.shape[0]
    points = truth_ref.shape[1]
    total = every_ref.shape[0]
    per = LANES // head_size
    groups = width // LANES
    scale = head_size ** (-0.5)
    factor = area_ref[...] * var_ref[...]
    head = lax.broadcasted_iota(jnp.int32, (points, width), 1) // head_size % per
    for m in range(members):
        mine = mine_ref[m]
        miss = mine - truth_ref[...]
        first = miss * lax.rsqrt(1.0 + miss * miss) / total
        second = jnp.zeros_like(mine)
        for f in range(total):
            paired = mine - every_ref[f]
            second = second + paired * lax.rsqrt(1.0 + paired * paired)
        dpred = (factor * (first - second / (total * (total - 1)))).astype(BF16)
        d_attended = dot(dpred, wout_ref[...], TN).astype(BF16)
        for p in range(per):
            da_scr[m, p * points : (p + 1) * points, :] = jnp.where(
                head == p, d_attended, jnp.zeros_like(d_attended)
            )

    def probs_grad(m, j):
        cols = slice(j * LANES, (j + 1) * LANES)
        return dot(v_ref[m, :, cols], da_scr[m, :, cols], NT)

    steps = [(m, j) for j in range(groups) for m in range(members)]
    ahead = probs_grad(*steps[0])
    d_keys, d_values = [], []
    for i, (m, j) in enumerate(steps):
        cols = slice(j * LANES, (j + 1) * LANES)
        d_probs = ahead
        if i + 1 < len(steps):
            ahead = probs_grad(*steps[i + 1])
        weights = weight_ref[m, j].astype(F32)
        inner = jnp.sum(weights * d_probs, axis=0, keepdims=True)
        d_scores = (weights * scale * (d_probs - inner)).astype(BF16)
        d_keys.append(dot(d_scores, qm_ref[:, cols]))
        d_values.append(dot(weight_ref[m, j], da_scr[m, :, cols]))
        if m == members - 1:
            dk_scr[:, cols] = by_chunk(d_keys, early, capacity).astype(BF16)
            dv_scr[:, cols] = by_chunk(d_values, early, capacity).astype(BF16)
            dk_ref[:, cols] = by_chunk(d_keys, late, capacity).astype(BF16)
            dv_ref[:, cols] = by_chunk(d_values, late, capacity).astype(BF16)
            d_keys, d_values = [], []
    return_rows(dk_scr[...], dv_scr[...], wk_ref, wv_ref, out_refs)


def late_rows_kernel(wk_ref, wv_ref, dk_ref, dv_ref, *out_refs):
    return_rows(dk_ref[...], dv_ref[...], wk_ref, wv_ref, out_refs)


def first_sum_kernel(members, order, capacity, send_ref, me_ref, *refs):
    chunks = len(order)
    out_ref = refs[chunks]
    place = one_hot(send_ref, me_ref, order, out_ref.shape[1])
    back = jnp.concatenate([r[...] for r in refs[:chunks]], axis=0).astype(F32)
    for m in range(members):
        mine = of_member(back, m, members, chunks, capacity).astype(BF16)
        out_ref[m] = dot(place, mine)


def last_sum_kernel(members, order, capacity, send_ref, me_ref, before_ref, *refs):
    chunks = len(order)
    out_ref, sum_scr, sems = refs[chunks:]
    own_rows, width = out_ref.shape[1:]
    parts = sems.shape[1]
    part = width // parts
    place = one_hot(send_ref, me_ref, order, own_rows)
    back = jnp.concatenate([r[...] for r in refs[:chunks]], axis=0).astype(F32)
    mine = [
        of_member(back, m, members, chunks, capacity).astype(BF16) for m in range(members)
    ]
    sends = []
    for m in range(members):
        for p in range(parts):
            cols = slice(p * part, (p + 1) * part)
            sum_scr[m, :, cols] = before_ref[m, :, cols] + dot(place, mine[m][:, cols])
            there = pl.ds(p * part, part)
            send = pltpu.make_async_copy(
                sum_scr.at[m, :, there], out_ref.at[m, :, there], sems.at[m, p]
            )
            send.start()
            sends.append(send)
    for send in sends:
        send.wait()


def last_sum(members, order, capacity, send_rows, me, before, blocks):
    step, width = blocks[0].shape
    own_rows = before.shape[1]
    parts = 4 if width % (4 * LANES) == 0 else 1
    moved = len(order) * step * width * 2 + 2 * members * own_rows * width * 4
    return pl.pallas_call(
        functools.partial(last_sum_kernel, members, order, capacity),
        out_shape=jax.ShapeDtypeStruct((members, own_rows, width), F32),
        in_specs=[VMEM, SMEM] + [VMEM] * (1 + len(order)),
        out_specs=pl.BlockSpec(memory_space=pltpu.HBM),
        scratch_shapes=[
            pltpu.VMEM((members, own_rows, width), F32),
            pltpu.SemaphoreType.DMA((members, parts)),
        ],
        compiler_params=pltpu.CompilerParams(vmem_limit_bytes=2 * moved + 2 * ROOM),
        cost_estimate=pl.CostEstimate(
            flops=2 * len(order) * step * own_rows * width,
            bytes_accessed=moved,
            transcendentals=0,
        ),
    )(send_rows, me, before, *blocks)


def on_device(
    chunks,
    latent,
    grid_feat,
    w_query,
    w_key,
    w_value,
    w_out,
    truth,
    area,
    var_weight,
    send_rows,
    neighbours,
    live_count,
):
    members, own_rows, width = latent.shape
    points, slots = neighbours.shape
    variables = w_out.shape[0]
    capacity = send_rows.shape[2]
    head_size = width // H
    per = LANES // head_size
    groups = width // LANES
    step = members * capacity
    received = chunks * capacity
    me = lax.axis_index("grid")
    half, quarter = chunks // 2, chunks // 4
    order = tuple(range(chunks))
    near, far = order[:half], order[half:]
    early = (0, *far[:quarter], *near[1 : max(quarter, 1)])
    late = tuple(s for s in [*far, *near] if s not in early)
    here = me[None]
    partners = jnp.bitwise_xor(me, jnp.arange(chunks, dtype=jnp.int32))

    def exchanged(blocks, masks):
        return [
            b if s == 0 else lax.ppermute(b, "grid", [(i, i ^ s) for i in range(chunks)])
            for s, b in zip(masks, blocks)
        ]

    chunk_shape = jax.ShapeDtypeStruct((step, width), BF16)
    outgoing = call(
        functools.partial(gather_kernel, members, order, capacity),
        [chunk_shape] * chunks,
        [latent, send_rows, here],
        flops=2 * members * received * own_rows * width,
        scalars=(2,),
        limit=40 * 1024 * 1024,
    )
    arrived_near = exchanged(outgoing[:half], near)
    arrived_far = exchanged(outgoing[half:], far)
    query = call(
        functools.partial(query_kernel, head_size),
        jax.ShapeDtypeStruct((per * points, width), BF16),
        [grid_feat, w_query],
        flops=2 * points * width * width,
    )
    row_ids = (partners[:, None] * capacity + jnp.arange(capacity, dtype=jnp.int32)).reshape(-1)
    live = jnp.arange(slots)[:, None] < live_count[None, :]
    names = jnp.where(live, neighbours.T, -1)
    mult = jnp.sum((row_ids[None, :, None] == names[:, None, :]).astype(F32), axis=0)

    raised, values_near = call(
        functools.partial(near_kernel, members, half, capacity, head_size),
        [
            jax.ShapeDtypeStruct((members, groups, half * capacity, per * points), F32),
            jax.ShapeDtypeStruct((members, half * capacity, width), BF16),
        ],
        [query, w_key, w_value, mult[: half * capacity], *arrived_near],
        scratch=[pltpu.VMEM((members, half * capacity, width), BF16)],
        flops=4 * members * half * capacity * width * width,
    )
    predicted, weights, values = call(
        functools.partial(forward_kernel, members, (chunks - half), capacity, head_size),
        [
            jax.ShapeDtypeStruct((members, variables, points), F32),
            jax.ShapeDtypeStruct((members, groups, received, per * points), BF16),
            jax.ShapeDtypeStruct((members, received, width), BF16),
        ],
        [query, w_key, w_value, w_out, mult, raised, values_near, *arrived_far],
        scratch=[
            pltpu.VMEM((members, (chunks - half) * capacity, width), BF16),
            pltpu.VMEM((width, points), BF16),
        ],
        flops=4 * members * (chunks - half) * capacity * width * width,
    )
    everyone = lax.all_gather(predicted, "member", axis=0, tiled=True)
    late_grad = jax.ShapeDtypeStruct((len(late) * step, width), BF16)
    *leaving_early, d_keys, d_values = call(
        functools.partial(
            backward_kernel, members, early, late, capacity, head_size
        ),
        [chunk_shape] * len(early) + [late_grad] * 2,
        [
            query,
            w_key,
            w_value,
            w_out,
            everyone,
            predicted,
            truth,
            area[None, :],
            var_weight[:, None],
            weights,
            values,
        ],
        scratch=[
            pltpu.VMEM((members, per * points, width), BF16),
            pltpu.VMEM((len(early) * step, width), BF16),
            pltpu.VMEM((len(early) * step, width), BF16),
        ],
        flops=4 * members * received * width * width,
    )
    returned_early = exchanged(leaving_early, early)
    leaving_late = call(
        late_rows_kernel,
        [chunk_shape] * len(late),
        [w_key, w_value, d_keys, d_values],
        flops=4 * len(late) * step * width * width,
    )
    returned_late = exchanged(leaving_late, late)
    before = call(
        functools.partial(first_sum_kernel, members, early, capacity),
        jax.ShapeDtypeStruct((members, own_rows, width), F32),
        [send_rows, here, *returned_early],
        flops=2 * len(early) * step * own_rows * width,
        scalars=(1,),
    )
    return last_sum(members, late, capacity, send_rows, here, before, returned_late)


def solution(mesh):
    return jax.shard_map(
        functools.partial(on_device, mesh.shape["grid"]),
        mesh=mesh,
        in_specs=(
            P("member", "grid", None),
            P("grid", None),
            P(),
            P(),
            P(),
            P(),
            P(None, "grid"),
            P("grid"),
            P(),
            P("grid", None, None),
            P("grid", None),
            P("grid"),
        ),
        out_specs=P("member", "grid", None),
        check_vma=False,
    )
```

```python
import functools
import math

import jax
import jax.numpy as jnp
import numpy as np
from jax import lax
from jax.experimental import pallas as pl
from jax.experimental.pallas import tpu as pltpu
from jax.sharding import PartitionSpec as P

H = 16
LANES = 128
ROOM = 4 * 1024 * 1024
WEIGHT = 40
F32 = jnp.float32
HUGE = float(np.finfo(np.float32).max)
BF16 = jnp.bfloat16
NN = (((1,), (0,)), ((), ()))
NT = (((1,), (1,)), ((), ()))
TN = (((0,), (0,)), ((), ()))
VMEM = pl.BlockSpec(memory_space=pltpu.VMEM)
SMEM = pl.BlockSpec(memory_space=pltpu.SMEM)


def dot(a, b, dims=NN):
    return lax.dot_general(a, b, dims, preferred_element_type=F32)


def call(kernel, out_shape, operands, scratch=(), flops=0, scalars=(), limit=None):
    single = not isinstance(out_shape, (list, tuple))
    outs = [out_shape] if single else out_shape
    moved = sum(x.size * x.dtype.itemsize for x in [*operands, *outs])
    held = sum(math.prod(s.shape) * jnp.dtype(s.dtype).itemsize for s in scratch)
    return pl.pallas_call(
        kernel,
        out_shape=out_shape,
        in_specs=[SMEM if i in scalars else VMEM for i in range(len(operands))],
        out_specs=VMEM if single else [VMEM] * len(outs),
        scratch_shapes=list(scratch),
        compiler_params=pltpu.CompilerParams(vmem_limit_bytes=limit or moved + 2 * held + ROOM),
        cost_estimate=pl.CostEstimate(flops=WEIGHT * flops, bytes_accessed=moved, transcendentals=0),
    )(*operands)


def of_member(block, member, members, chunks, capacity):
    step = members * capacity
    first = member * capacity
    return jnp.concatenate(
        [block[c * step + first : c * step + first + capacity] for c in range(chunks)], axis=0
    )


def by_chunk(blocks, chunks, capacity):
    return jnp.concatenate(
        [b[c * capacity : (c + 1) * capacity] for c in chunks for b in blocks], axis=0
    )


def named_rows(send_ref, me_ref, order):
    return jnp.concatenate(
        [
            send_ref[0, pl.ds(lax.rem(me_ref[0] + shift, send_ref.shape[1]), 1), :]
            for shift in order
        ],
        axis=1,
    )


def one_hot(send_ref, me_ref, order, own_rows):
    rows = named_rows(send_ref, me_ref, order)
    ids = lax.broadcasted_iota(jnp.int32, (own_rows, rows.shape[1]), 0)
    return (rows == ids).astype(F32).astype(BF16)


def gather_kernel(members, order, capacity, latent_ref, send_ref, me_ref, *out_refs):
    chunks = len(order)
    pick = one_hot(send_ref, me_ref, order, latent_ref.shape[1])
    picked = [dot(pick, latent_ref[m], TN) for m in range(members)]
    step = members * capacity
    rows = by_chunk(picked, range(chunks), capacity).astype(BF16)
    for c in range(chunks):
        out_refs[c][...] = rows[c * step : (c + 1) * step]


def query_kernel(
    order, capacity, head_size, feat_ref, w_ref, names_ref, live_ref, me_ref, out_ref, mult_ref
):
    points, width = feat_ref.shape
    slots = names_ref.shape[0]
    per = LANES // head_size
    query = dot(feat_ref[...], w_ref[...]).astype(BF16)
    head = lax.broadcasted_iota(jnp.int32, (points, width), 1) // head_size % per
    for p in range(per):
        out_ref[p * points : (p + 1) * points, :] = jnp.where(
            head == p, query, jnp.zeros_like(query)
        )
    place = lax.broadcasted_iota(jnp.int32, (capacity, points), 0)
    owners = [lax.rem(me_ref[0] + len(order) - shift, len(order)) for shift in order]
    ids = jnp.concatenate([place + owner * capacity for owner in owners], axis=0)
    mult = jnp.zeros(ids.shape, F32)
    for k in range(slots):
        name = jnp.where(live_ref[...] > k, names_ref[k : k + 1, :], -1)
        mult = mult + jnp.where(ids == name, 1.0, 0.0)
    mult_ref[...] = mult


def project(rows, wk_ref, wv_ref, k_scr, v_ref, offset, members, chunks, capacity):
    width = wk_ref.shape[0]
    tile = 2 * LANES
    rows_here = pl.ds(offset, chunks * capacity)
    for t in range(width // tile):
        cols = slice(t * tile, (t + 1) * tile)
        keys = dot(rows, wk_ref[:, cols])
        values = dot(rows, wv_ref[:, cols])
        for m in range(members):
            k_scr[m, :, cols] = of_member(keys, m, members, chunks, capacity).astype(BF16)
            v_ref[m, rows_here, cols] = of_member(values, m, members, chunks, capacity).astype(
                BF16
            )


def raised_scores(k_scr, qm_ref, m, j, factor, bias, mult):
    cols = slice(j * LANES, (j + 1) * LANES)
    raised = jnp.exp2(dot(k_scr[m, :, cols], qm_ref[:, cols], NT) * factor + bias)
    raised = jnp.minimum(mult * raised, HUGE)
    return raised, jnp.sum(raised, axis=0, keepdims=True)


def exponent(head_size):
    return head_size ** (-0.5) * math.log2(math.e)


def near_kernel(members, chunks, capacity, head_size, qm_ref, wk_ref, wv_ref, mult_ref, *refs):
    raised_ref, total_ref, v_ref, k_scr = refs[chunks:]
    groups = wk_ref.shape[0] // LANES
    rows = jnp.concatenate([r[...] for r in refs[:chunks]], axis=0)
    project(rows, wk_ref, wv_ref, k_scr, v_ref, 0, members, chunks, capacity)
    mult = mult_ref[: k_scr.shape[1], :]
    mult = jnp.concatenate([mult] * (LANES // head_size), axis=1)
    bias = jnp.where(mult > 0.0, 0.0, -jnp.inf)
    for m in range(members):
        for j in range(groups):
            raised_ref[m, j], total_ref[m, j] = raised_scores(
                k_scr, qm_ref, m, j, exponent(head_size), bias, mult
            )


def forward_kernel(
    members,
    chunks,
    capacity,
    head_size,
    qm_ref,
    wk_ref,
    wv_ref,
    wout_ref,
    mult_ref,
    raised_ref,
    total_ref,
    v_near_ref,
    *refs,
):
    pred_ref, weight_ref, v_ref, k_scr, att_scr = refs[chunks:]
    points = mult_ref.shape[1]
    per = LANES // head_size
    groups = wk_ref.shape[0] // LANES
    done = v_near_ref.shape[1]
    rows = jnp.concatenate([r[...] for r in refs[:chunks]], axis=0)
    v_ref[:, :done, :] = v_near_ref[...]
    project(rows, wk_ref, wv_ref, k_scr, v_ref, done, members, chunks, capacity)
    mult = jnp.concatenate([mult_ref[done:, :]] * per, axis=1)
    bias = jnp.where(mult > 0.0, 0.0, -jnp.inf)
    steps = [(m, j) for m in range(members) for j in range(groups)]
    ahead = raised_scores(k_scr, qm_ref, *steps[0], exponent(head_size), bias, mult)
    for i, (m, j) in enumerate(steps):
        late, late_total = ahead
        raised = jnp.concatenate([raised_ref[m, j], late], axis=0)
        root = lax.rsqrt(total_ref[m, j] + late_total)
        if i + 1 < len(steps):
            ahead = raised_scores(
                k_scr, qm_ref, *steps[i + 1], exponent(head_size), bias, mult
            )
        weights = (raised * root * root).astype(BF16)
        weight_ref[m, j] = weights
        both = dot(v_ref[m, :, j * LANES : (j + 1) * LANES], weights, TN)
        for p in range(per):
            first = p * head_size
            att_scr[pl.ds(j * LANES + first, head_size), :] = both[
                first : first + head_size, p * points : (p + 1) * points
            ].astype(BF16)
        if j == groups - 1:
            pred_ref[m] = dot(wout_ref[...], att_scr[...])


def transpose_kernel(a_ref, b_ref, at_ref, bt_ref):
    at_ref[...] = a_ref[...].T
    bt_ref[...] = b_ref[...].T


def return_rows(dk, dv, wkt_ref, wvt_ref, out_refs):
    width = wkt_ref.shape[1]
    tile = 2 * LANES
    step = out_refs[0].shape[0]
    for t in range(width // tile):
        cols = slice(t * tile, (t + 1) * tile)
        rows = dot(dk, wkt_ref[:, cols]) + dot(dv, wvt_ref[:, cols])
        rows = rows.astype(BF16)
        for c, out_ref in enumerate(out_refs):
            out_ref[:, cols] = rows[c * step : (c + 1) * step]


def backward_kernel(
    members,
    early,
    late,
    capacity,
    head_size,
    qm_ref,
    wkt_ref,
    wvt_ref,
    wout_ref,
    mine_ref,
    truth_ref,
    area_ref,
    var_ref,
    weight_ref,
    v_ref,
    *refs,
):
    other_refs = refs[: len(refs) - len(early) - 5]
    out_refs = refs[len(other_refs) : -5]
    dk_ref, dv_ref, da_scr, dk_scr, dv_scr = refs[-5:]
    width = wkt_ref.shape[1]
    points = truth_ref.shape[1]
    every_refs = (mine_ref, *other_refs)
    total = sum(r.shape[0] for r in every_refs)
    per = LANES // head_size
    groups = width // LANES
    scale = head_size ** (-0.5)
    variables = var_ref.shape[1]
    wide = -variables % LANES
    var = jnp.concatenate([var_ref[...], jnp.zeros((1, wide), F32)], axis=1)
    var = jnp.broadcast_to(var, (LANES, variables + wide)).T[:variables, :1]
    factor = area_ref[...] * var
    head = lax.broadcasted_iota(jnp.int32, (points, width), 1) // head_size % per
    for m in range(members):
        mine = mine_ref[m]
        miss = mine - truth_ref[...]
        first = miss * lax.rsqrt(1.0 + miss * miss) / total
        second = jnp.zeros_like(mine)
        for every_ref in every_refs:
            for f in range(every_ref.shape[0]):
                paired = mine - every_ref[f]
                second = second + paired * lax.rsqrt(1.0 + paired * paired)
        dpred = (factor * (first - second / (total * (total - 1)))).astype(BF16)
        d_attended = dot(dpred, wout_ref[...], TN).astype(BF16)
        for p in range(per):
            da_scr[m, p * points : (p + 1) * points, :] = jnp.where(
                head == p, d_attended, jnp.zeros_like(d_attended)
            )

    def probs_grad(m, j):
        cols = slice(j * LANES, (j + 1) * LANES)
        return dot(v_ref[m, :, cols], da_scr[m, :, cols], NT)

    steps = [(m, j) for j in range(groups) for m in range(members)]
    ahead = probs_grad(*steps[0])
    d_keys, d_values = [], []
    for i, (m, j) in enumerate(steps):
        cols = slice(j * LANES, (j + 1) * LANES)
        d_probs = ahead
        if i + 1 < len(steps):
            ahead = probs_grad(*steps[i + 1])
        weights = weight_ref[m, j].astype(F32)
        inner = jnp.sum(weights * d_probs, axis=0, keepdims=True)
        d_scores = (weights * (d_probs - inner)).astype(BF16)
        d_keys.append(dot(d_scores, qm_ref[:, cols]) * scale)
        d_values.append(dot(weight_ref[m, j], da_scr[m, :, cols]))
        if m == members - 1:
            dk_scr[:, cols] = by_chunk(d_keys, early, capacity).astype(BF16)
            dv_scr[:, cols] = by_chunk(d_values, early, capacity).astype(BF16)
            dk_ref[:, cols] = by_chunk(d_keys, late, capacity).astype(BF16)
            dv_ref[:, cols] = by_chunk(d_values, late, capacity).astype(BF16)
            d_keys, d_values = [], []
    return_rows(dk_scr[...], dv_scr[...], wkt_ref, wvt_ref, out_refs)


def late_rows_kernel(wkt_ref, wvt_ref, dk_ref, dv_ref, *out_refs):
    return_rows(dk_ref[...], dv_ref[...], wkt_ref, wvt_ref, out_refs)


def first_sum_kernel(members, order, capacity, send_ref, me_ref, *refs):
    chunks = len(order)
    out_ref = refs[chunks]
    place = one_hot(send_ref, me_ref, order, out_ref.shape[1])
    back = jnp.concatenate([r[...] for r in refs[:chunks]], axis=0).astype(F32)
    for m in range(members):
        mine = of_member(back, m, members, chunks, capacity).astype(BF16)
        out_ref[m] = dot(place, mine)


def last_sum_kernel(members, order, capacity, send_ref, me_ref, before_ref, *refs):
    chunks = len(order)
    out_ref, sum_scr, sems = refs[chunks:]
    own_rows, width = out_ref.shape[1:]
    parts = sems.shape[1]
    part = width // parts
    place = one_hot(send_ref, me_ref, order, own_rows)
    back = jnp.concatenate([r[...] for r in refs[:chunks]], axis=0).astype(F32)
    mine = [
        of_member(back, m, members, chunks, capacity).astype(BF16) for m in range(members)
    ]
    sends = []
    for m in range(members):
        for p in range(parts):
            cols = slice(p * part, (p + 1) * part)
            sum_scr[m, :, cols] = before_ref[m, :, cols] + dot(place, mine[m][:, cols])
            there = pl.ds(p * part, part)
            send = pltpu.make_async_copy(
                sum_scr.at[m, :, there], out_ref.at[m, :, there], sems.at[m, p]
            )
            send.start()
            sends.append(send)
    for send in sends:
        send.wait()


def last_sum(members, order, capacity, send_rows, me, before, blocks):
    step, width = blocks[0].shape
    own_rows = before.shape[1]
    parts = 4 if width % (4 * LANES) == 0 else 1
    moved = len(order) * step * width * 2 + 2 * members * own_rows * width * 4
    return pl.pallas_call(
        functools.partial(last_sum_kernel, members, order, capacity),
        out_shape=jax.ShapeDtypeStruct((members, own_rows, width), F32),
        in_specs=[VMEM, SMEM] + [VMEM] * (1 + len(order)),
        out_specs=pl.BlockSpec(memory_space=pltpu.HBM),
        scratch_shapes=[
            pltpu.VMEM((members, own_rows, width), F32),
            pltpu.SemaphoreType.DMA((members, parts)),
        ],
        compiler_params=pltpu.CompilerParams(vmem_limit_bytes=2 * moved + 2 * ROOM),
        cost_estimate=pl.CostEstimate(
            flops=2 * len(order) * step * own_rows * width,
            bytes_accessed=moved,
            transcendentals=0,
        ),
    )(send_rows, me, before, *blocks)


def shifts_from(chunks, first):
    return tuple(dict.fromkeys([0, *(s % chunks for s in first), *range(chunks)]))


def on_device(
    chunks,
    ensembles,
    latent,
    grid_feat,
    w_query,
    w_key,
    w_value,
    w_out,
    truth,
    area,
    var_weight,
    send_rows,
    neighbours,
    live_count,
):
    members, own_rows, width = latent.shape
    points, slots = neighbours.shape
    variables = w_out.shape[0]
    capacity = send_rows.shape[2]
    head_size = width // H
    per = LANES // head_size
    groups = width // LANES
    step = members * capacity
    received = chunks * capacity
    me = lax.axis_index("grid")
    half = chunks // 2
    order = shifts_from(chunks, (1, -1, half, half - 1, half + 1, 2, -2))
    near, far = order[:half], order[half:]
    leave = shifts_from(chunks, (half, half - 1, half + 1, 1, 2, -2, -1))
    early, late = leave[:half], leave[half:]
    here = me[None]

    def exchanged(blocks, shifts, sign):
        return [
            b
            if s == 0
            else lax.ppermute(b, "grid", [(i, (i + sign * s) % chunks) for i in range(chunks)])
            for s, b in zip(shifts, blocks)
        ]

    chunk_shape = jax.ShapeDtypeStruct((step, width), BF16)
    outgoing = call(
        functools.partial(gather_kernel, members, order, capacity),
        [chunk_shape] * chunks,
        [latent, send_rows, here],
        flops=2 * members * received * own_rows * width,
        scalars=(2,),
        limit=40 * 1024 * 1024,
    )
    arrived_near = exchanged(outgoing[: len(near)], near, 1)
    arrived_far = exchanged(outgoing[len(near) :], far, 1)
    query, mult = call(
        functools.partial(query_kernel, order, capacity, head_size),
        [
            jax.ShapeDtypeStruct((per * points, width), BF16),
            jax.ShapeDtypeStruct((received, points), F32),
        ],
        [grid_feat, w_query, neighbours.T, live_count[None, :], here],
        flops=2 * points * width * width,
        scalars=(4,),
    )

    raised, totals, values_near = call(
        functools.partial(near_kernel, members, len(near), capacity, head_size),
        [
            jax.ShapeDtypeStruct((members, groups, len(near) * capacity, per * points), F32),
            jax.ShapeDtypeStruct((members, groups, 1, per * points), F32),
            jax.ShapeDtypeStruct((members, len(near) * capacity, width), BF16),
        ],
        [query, w_key, w_value, mult, *arrived_near],
        scratch=[pltpu.VMEM((members, len(near) * capacity, width), BF16)],
        flops=4 * members * len(near) * capacity * width * width,
    )
    predicted, weights, values = call(
        functools.partial(forward_kernel, members, len(far), capacity, head_size),
        [
            jax.ShapeDtypeStruct((members, variables, points), F32),
            jax.ShapeDtypeStruct((members, groups, received, per * points), BF16),
            jax.ShapeDtypeStruct((members, received, width), BF16),
        ],
        [query, w_key, w_value, w_out, mult, raised, totals, values_near, *arrived_far],
        scratch=[
            pltpu.VMEM((members, len(far) * capacity, width), BF16),
            pltpu.VMEM((width, points), BF16),
        ],
        flops=4 * members * len(far) * capacity * width * width,
    )
    everyone = [predicted]
    bit = ensembles // 2
    while bit:
        pairs = [(i, i ^ bit) for i in range(ensembles)]
        everyone += [lax.ppermute(p, "member", pairs) for p in everyone]
        bit //= 2
    w_key_t, w_value_t = call(
        transpose_kernel,
        [jax.ShapeDtypeStruct((width, width), BF16)] * 2,
        [w_key, w_value],
        flops=width * width,
    )
    late_grad = jax.ShapeDtypeStruct((len(late) * step, width), BF16)
    *leaving_early, d_keys, d_values = call(
        functools.partial(
            backward_kernel, members, [order.index(c) for c in early], [order.index(c) for c in late], capacity, head_size
        ),
        [chunk_shape] * len(early) + [late_grad] * 2,
        [
            query,
            w_key_t,
            w_value_t,
            w_out,
            predicted,
            truth,
            area[None, :],
            var_weight[None, :],
            weights,
            values,
            *everyone[1:],
        ],
        scratch=[
            pltpu.VMEM((members, per * points, width), BF16),
            pltpu.VMEM((len(early) * step, width), BF16),
            pltpu.VMEM((len(early) * step, width), BF16),
        ],
        flops=4 * members * received * width * width,
    )
    returned_early = exchanged(leaving_early, early, -1)
    leaving_late = call(
        late_rows_kernel,
        [chunk_shape] * len(late),
        [w_key_t, w_value_t, d_keys, d_values],
        flops=4 * len(late) * step * width * width,
    )
    returned_late = exchanged(leaving_late, late, -1)
    before = call(
        functools.partial(first_sum_kernel, members, early, capacity),
        jax.ShapeDtypeStruct((members, own_rows, width), F32),
        [send_rows, here, *returned_early],
        flops=2 * len(early) * step * own_rows * width,
        scalars=(1,),
    )
    return last_sum(members, late, capacity, send_rows, here, before, returned_late)


def solution(mesh):
    return jax.shard_map(
        functools.partial(on_device, mesh.shape["grid"], mesh.shape["member"]),
        mesh=mesh,
        in_specs=(
            P("member", "grid", None),
            P("grid", None),
            P(),
            P(),
            P(),
            P(),
            P(None, "grid"),
            P("grid"),
            P(),
            P("grid", None, None),
            P("grid", None),
            P("grid"),
        ),
        out_specs=P("member", "grid", None),
        check_vma=False,
    )
```

```python
import functools
import math

import jax
import jax.numpy as jnp
import numpy as np
from jax import lax
from jax.experimental import pallas as pl
from jax.experimental.pallas import tpu as pltpu
from jax.sharding import PartitionSpec as P

H = 16
LANES = 128
ROOM = 4 * 1024 * 1024
WEIGHT = 40
F32 = jnp.float32
HUGE = float(np.finfo(np.float32).max)
BF16 = jnp.bfloat16
NN = (((1,), (0,)), ((), ()))
NT = (((1,), (1,)), ((), ()))
TN = (((0,), (0,)), ((), ()))
VMEM = pl.BlockSpec(memory_space=pltpu.VMEM)
SMEM = pl.BlockSpec(memory_space=pltpu.SMEM)


def dot(a, b, dims=NN):
    return lax.dot_general(a, b, dims, preferred_element_type=F32)


def call(kernel, out_shape, operands, scratch=(), flops=0, scalars=(), limit=None):
    single = not isinstance(out_shape, (list, tuple))
    outs = [out_shape] if single else out_shape
    moved = sum(x.size * x.dtype.itemsize for x in [*operands, *outs])
    held = sum(math.prod(s.shape) * jnp.dtype(s.dtype).itemsize for s in scratch)
    return pl.pallas_call(
        kernel,
        out_shape=out_shape,
        in_specs=[SMEM if i in scalars else VMEM for i in range(len(operands))],
        out_specs=VMEM if single else [VMEM] * len(outs),
        scratch_shapes=list(scratch),
        compiler_params=pltpu.CompilerParams(vmem_limit_bytes=limit or moved + 2 * held + ROOM),
        cost_estimate=pl.CostEstimate(flops=WEIGHT * flops, bytes_accessed=moved, transcendentals=0),
    )(*operands)


def of_member(block, member, members, chunks, capacity):
    step = members * capacity
    first = member * capacity
    return jnp.concatenate(
        [block[c * step + first : c * step + first + capacity] for c in range(chunks)], axis=0
    )


def by_chunk(blocks, chunks, capacity):
    return jnp.concatenate(
        [b[c * capacity : (c + 1) * capacity] for c in chunks for b in blocks], axis=0
    )


def named_rows(send_ref, me_ref, order):
    return jnp.concatenate(
        [
            send_ref[0, pl.ds(lax.rem(me_ref[0] + shift, send_ref.shape[1]), 1), :]
            for shift in order
        ],
        axis=1,
    )


def one_hot(send_ref, me_ref, order, own_rows):
    rows = named_rows(send_ref, me_ref, order)
    ids = lax.broadcasted_iota(jnp.int32, (own_rows, rows.shape[1]), 0)
    return (rows == ids).astype(F32).astype(BF16)


def of_chunks(block, chunks, capacity):
    return jnp.concatenate(
        [block[c * capacity : (c + 1) * capacity] for c in chunks], axis=0
    )


def ids_kernel(out_ref):
    out_ref[...] = lax.broadcasted_iota(jnp.int32, out_ref.shape, 0)


def pick_kernel(order, send_ref, me_ref, ids_ref, out_ref):
    rows = named_rows(send_ref, me_ref, order)
    out_ref[...] = (rows == ids_ref[...]).astype(F32).astype(BF16)


def one_hot_kernel(orders, send_ref, me_ref, *out_refs):
    for order, out_ref in zip(orders, out_refs):
        out_ref[...] = one_hot(send_ref, me_ref, order, out_ref.shape[0])


def gather_kernel(members, chunks, capacity, latent_ref, pick_ref, *out_refs):
    picked = [dot(pick_ref[...], latent_ref[m], TN) for m in range(members)]
    step = members * capacity
    rows = by_chunk(picked, range(chunks), capacity).astype(BF16)
    for c in range(chunks):
        out_refs[c][...] = rows[c * step : (c + 1) * step]


def query_kernel(
    order, capacity, head_size, feat_ref, w_ref, names_ref, live_ref, me_ref, out_ref, mult_ref
):
    points, width = feat_ref.shape
    slots = names_ref.shape[0]
    per = LANES // head_size
    query = dot(feat_ref[...], w_ref[...]).astype(BF16)
    head = lax.broadcasted_iota(jnp.int32, (points, width), 1) // head_size % per
    for p in range(per):
        out_ref[p * points : (p + 1) * points, :] = jnp.where(
            head == p, query, jnp.zeros_like(query)
        )
    place = lax.broadcasted_iota(jnp.int32, (capacity, points), 0)
    owners = [lax.rem(me_ref[0] + len(order) - shift, len(order)) for shift in order]
    ids = jnp.concatenate([place + owner * capacity for owner in owners], axis=0)
    mult = jnp.zeros(ids.shape, F32)
    for k in range(slots):
        name = jnp.where(live_ref[...] > k, names_ref[k : k + 1, :], -1)
        mult = mult + jnp.where(ids == name, 1.0, 0.0)
    mult_ref[...] = mult


def project(rows, wk_ref, wv_ref, k_scr, v_ref, offset, members, chunks, capacity):
    width = wk_ref.shape[0]
    tile = 2 * LANES
    rows_here = pl.ds(offset, chunks * capacity)
    for t in range(width // tile):
        cols = slice(t * tile, (t + 1) * tile)
        keys = dot(rows, wk_ref[:, cols])
        values = dot(rows, wv_ref[:, cols])
        for m in range(members):
            k_scr[m, :, cols] = of_member(keys, m, members, chunks, capacity).astype(BF16)
            v_ref[m, rows_here, cols] = of_member(values, m, members, chunks, capacity).astype(
                BF16
            )


def raised_scores(k_scr, qm_ref, m, j, factor, bias, mult):
    cols = slice(j * LANES, (j + 1) * LANES)
    raised = jnp.exp2(dot(k_scr[m, :, cols], qm_ref[:, cols], NT) * factor + bias)
    raised = jnp.minimum(mult * raised, HUGE)
    return raised, jnp.sum(raised, axis=0, keepdims=True)


def exponent(head_size):
    return head_size ** (-0.5) * math.log2(math.e)


def near_kernel(
    members, chunks, capacity, head_size, before, qm_ref, wk_ref, wv_ref, mult_ref, *refs
):
    raised_ref, total_ref, v_ref, k_scr = refs[chunks:]
    groups = wk_ref.shape[0] // LANES
    rows = jnp.concatenate([r[...] for r in refs[:chunks]], axis=0)
    project(rows, wk_ref, wv_ref, k_scr, v_ref, 0, members, chunks, capacity)
    mult = mult_ref[before : before + k_scr.shape[1], :]
    mult = jnp.concatenate([mult] * (LANES // head_size), axis=1)
    bias = jnp.where(mult > 0.0, 0.0, -jnp.inf)
    for m in range(members):
        for j in range(groups):
            raised_ref[m, j], total_ref[m, j] = raised_scores(
                k_scr, qm_ref, m, j, exponent(head_size), bias, mult
            )


def forward_kernel(
    members,
    chunks,
    capacity,
    head_size,
    qm_ref,
    wk_ref,
    wv_ref,
    wout_ref,
    mult_ref,
    *refs,
):
    pred_ref, weight_ref, v_ref, k_scr, att_scr = refs[-5:]
    chunk_refs = refs[-5 - chunks : -5]
    parts = refs[: -5 - chunks]
    raised_refs, total_refs, v_refs = parts[0::3], parts[1::3], parts[2::3]
    points = mult_ref.shape[1]
    per = LANES // head_size
    groups = wk_ref.shape[0] // LANES
    done = 0
    for v_part in v_refs:
        v_ref[:, done : done + v_part.shape[1], :] = v_part[...]
        done += v_part.shape[1]
    rows = jnp.concatenate([r[...] for r in chunk_refs], axis=0)
    project(rows, wk_ref, wv_ref, k_scr, v_ref, done, members, chunks, capacity)
    mult = jnp.concatenate([mult_ref[done:, :]] * per, axis=1)
    bias = jnp.where(mult > 0.0, 0.0, -jnp.inf)
    steps = [(m, j) for m in range(members) for j in range(groups)]
    ahead = raised_scores(k_scr, qm_ref, *steps[0], exponent(head_size), bias, mult)
    for i, (m, j) in enumerate(steps):
        late, late_total = ahead
        raised = jnp.concatenate([r[m, j] for r in raised_refs] + [late], axis=0)
        root = lax.rsqrt(sum([t[m, j] for t in total_refs], late_total))
        if i + 1 < len(steps):
            ahead = raised_scores(
                k_scr, qm_ref, *steps[i + 1], exponent(head_size), bias, mult
            )
        weights = (raised * root * root).astype(BF16)
        weight_ref[m, j] = weights
        both = dot(v_ref[m, :, j * LANES : (j + 1) * LANES], weights, TN)
        for p in range(per):
            first = p * head_size
            att_scr[pl.ds(j * LANES + first, head_size), :] = both[
                first : first + head_size, p * points : (p + 1) * points
            ].astype(BF16)
        if j == groups - 1:
            pred_ref[m] = dot(wout_ref[...], att_scr[...])


def first_kernel(sizes, orders, qm_ref, wk_ref, wv_ref, mult_ref, send_ref, me_ref, *refs):
    *refs, k_scr = refs
    last = len(refs) - 2 - len(orders)
    wkt_ref, wvt_ref, *place_refs = refs[last:]
    near_kernel(*sizes, qm_ref, wk_ref, wv_ref, mult_ref, *refs[:last], k_scr)
    wkt_ref[...] = wk_ref[...].T
    wvt_ref[...] = wv_ref[...].T
    one_hot_kernel(orders, send_ref, me_ref, *place_refs)


def return_rows(dk, dv, wkt_ref, wvt_ref, out_refs):
    width = wkt_ref.shape[1]
    tile = 2 * LANES
    step = out_refs[0].shape[0]
    for t in range(width // tile):
        cols = slice(t * tile, (t + 1) * tile)
        rows = dot(dk, wkt_ref[:, cols]) + dot(dv, wvt_ref[:, cols])
        rows = rows.astype(BF16)
        for c, out_ref in enumerate(out_refs):
            out_ref[:, cols] = rows[c * step : (c + 1) * step]


def backward_kernel(
    members,
    early,
    late,
    capacity,
    head_size,
    qm_ref,
    wkt_ref,
    wvt_ref,
    wout_ref,
    mine_ref,
    truth_ref,
    area_ref,
    var_ref,
    weight_ref,
    v_ref,
    *refs,
):
    other_refs = refs[: len(refs) - len(early) - 5]
    out_refs = refs[len(other_refs) : -5]
    ds_ref, w_ref, da_ref, dk_scr, dv_scr = refs[-5:]
    width = wkt_ref.shape[1]
    points = truth_ref.shape[1]
    every_refs = (mine_ref, *other_refs)
    total = sum(r.shape[0] for r in every_refs)
    per = LANES // head_size
    groups = width // LANES
    scale = head_size ** (-0.5)
    variables = var_ref.shape[1]
    wide = -variables % LANES
    var = jnp.concatenate([var_ref[...], jnp.zeros((1, wide), F32)], axis=1)
    var = jnp.broadcast_to(var, (LANES, variables + wide)).T[:variables, :1]
    factor = area_ref[...] * var
    head = lax.broadcasted_iota(jnp.int32, (points, width), 1) // head_size % per
    for m in range(members):
        mine = mine_ref[m]
        miss = mine - truth_ref[...]
        first = miss * lax.rsqrt(1.0 + miss * miss) / total
        second = jnp.zeros_like(mine)
        for every_ref in every_refs:
            for f in range(every_ref.shape[0]):
                paired = mine - every_ref[f]
                second = second + paired * lax.rsqrt(1.0 + paired * paired)
        dpred = (factor * (first - second / (total * (total - 1)))).astype(BF16)
        d_attended = dot(dpred, wout_ref[...], TN).astype(BF16)
        for p in range(per):
            da_ref[m, p * points : (p + 1) * points, :] = jnp.where(
                head == p, d_attended, jnp.zeros_like(d_attended)
            )

    def probs_grad(m, j):
        cols = slice(j * LANES, (j + 1) * LANES)
        return dot(v_ref[m, :, cols], da_ref[m, :, cols], NT)

    steps = [(m, j) for j in range(groups) for m in range(members)]
    ahead = probs_grad(*steps[0])
    d_keys, d_values = [], []
    for i, (m, j) in enumerate(steps):
        cols = slice(j * LANES, (j + 1) * LANES)
        d_probs = ahead
        if i + 1 < len(steps):
            ahead = probs_grad(*steps[i + 1])
        weights = weight_ref[m, j].astype(F32)
        inner = jnp.sum(weights * d_probs, axis=0, keepdims=True)
        d_scores = weights * (d_probs - inner)
        ds_ref[m, j] = of_chunks(d_scores, late, capacity).astype(BF16)
        w_ref[m, j] = of_chunks(weights, late, capacity).astype(BF16)
        now = of_chunks(d_scores, early, capacity).astype(BF16)
        d_keys.append(dot(now, qm_ref[:, cols]) * scale)
        now = of_chunks(weights, early, capacity).astype(BF16)
        d_values.append(dot(now, da_ref[m, :, cols]))
        if m == members - 1:
            dk_scr[:, cols] = by_chunk(d_keys, range(len(early)), capacity).astype(BF16)
            dv_scr[:, cols] = by_chunk(d_values, range(len(early)), capacity).astype(BF16)
            d_keys, d_values = [], []
    return_rows(dk_scr[...], dv_scr[...], wkt_ref, wvt_ref, out_refs)


def late_rows_kernel(
    chunks, capacity, head_size, qm_ref, wkt_ref, wvt_ref, ds_ref, w_ref, da_ref, *refs
):
    out_refs = refs[:chunks]
    dk_scr, dv_scr = refs[chunks:]
    members, groups = ds_ref.shape[:2]
    scale = head_size ** (-0.5)
    for j in range(groups):
        cols = slice(j * LANES, (j + 1) * LANES)
        d_keys = [dot(ds_ref[m, j], qm_ref[:, cols]) * scale for m in range(members)]
        d_values = [dot(w_ref[m, j], da_ref[m, :, cols]) for m in range(members)]
        dk_scr[:, cols] = by_chunk(d_keys, range(chunks), capacity).astype(BF16)
        dv_scr[:, cols] = by_chunk(d_values, range(chunks), capacity).astype(BF16)
    return_rows(dk_scr[...], dv_scr[...], wkt_ref, wvt_ref, out_refs)


def first_sum_kernel(members, capacity, place_ref, *refs):
    *_, out_ref = refs
    chunks = len(refs) - 1
    place = place_ref[...]
    back = jnp.concatenate([r[...] for r in refs[:chunks]], axis=0).astype(F32)
    for m in range(members):
        mine = of_member(back, m, members, chunks, capacity).astype(BF16)
        out_ref[m] = dot(place, mine)


def last_sum_kernel(members, capacity, place_ref, before_ref, *refs):
    chunks = len(refs) - 3
    out_ref, sum_scr, sems = refs[chunks:]
    parts = sems.shape[1]
    part = out_ref.shape[1] // parts
    back = jnp.concatenate([r[...] for r in refs[:chunks]], axis=0).astype(F32)
    mine = [
        of_member(back, m, members, chunks, capacity).astype(BF16) for m in range(members)
    ]
    sends = []
    for m in range(members):
        for p in range(parts):
            rows = slice(p * part, (p + 1) * part)
            sum_scr[m, rows, :] = before_ref[m, rows, :] + dot(place_ref[rows, :], mine[m])
            there = pl.ds(p * part, part)
            send = pltpu.make_async_copy(
                sum_scr.at[m, there], out_ref.at[m, there], sems.at[m, p]
            )
            send.start()
            sends.append(send)
    for send in sends:
        send.wait()


def last_sum(members, capacity, place, before, blocks):
    step, width = blocks[0].shape
    own_rows = before.shape[1]
    parts = next(p for p in (5, 4, 2, 1) if own_rows % (p * 16) == 0)
    moved = len(blocks) * step * width * 2 + 2 * members * own_rows * width * 4
    return pl.pallas_call(
        functools.partial(last_sum_kernel, members, capacity),
        out_shape=jax.ShapeDtypeStruct((members, own_rows, width), F32),
        in_specs=[VMEM] * (2 + len(blocks)),
        out_specs=pl.BlockSpec(memory_space=pltpu.HBM),
        scratch_shapes=[
            pltpu.VMEM((members, own_rows, width), F32),
            pltpu.SemaphoreType.DMA((members, parts)),
        ],
        compiler_params=pltpu.CompilerParams(vmem_limit_bytes=2 * moved + 2 * ROOM),
        cost_estimate=pl.CostEstimate(
            flops=2 * len(blocks) * step * own_rows * width,
            bytes_accessed=moved,
            transcendentals=0,
        ),
    )(place, before, *blocks)


def shifts_from(chunks, first):
    return tuple(dict.fromkeys([0, *(s % chunks for s in first), *range(chunks)]))


def on_device(
    chunks,
    ensembles,
    latent,
    grid_feat,
    w_query,
    w_key,
    w_value,
    w_out,
    truth,
    area,
    var_weight,
    send_rows,
    neighbours,
    live_count,
):
    members, own_rows, width = latent.shape
    points, slots = neighbours.shape
    variables = w_out.shape[0]
    capacity = send_rows.shape[2]
    head_size = width // H
    per = LANES // head_size
    groups = width // LANES
    step = members * capacity
    received = chunks * capacity
    me = lax.axis_index("grid")
    half = chunks // 2
    order = shifts_from(chunks, (half, 1, -1, half - 1, half + 1, 2, -2))
    groups_in = [order[:half], order[half:]]
    leave = shifts_from(chunks, (half, half - 1, half + 1, 1, 2, -2, -1))
    early, late = leave[:half], leave[half:]
    here = me[None]

    def exchanged(blocks, shifts, sign):
        return [
            b
            if s == 0
            else lax.ppermute(b, "grid", [(i, (i + sign * s) % chunks) for i in range(chunks)])
            for s, b in zip(shifts, blocks)
        ]

    chunk_shape = jax.ShapeDtypeStruct((step, width), BF16)
    ids = call(
        ids_kernel,
        jax.ShapeDtypeStruct((own_rows, received), jnp.int32),
        [],
        flops=members * received * own_rows * width,
    )
    pick = call(
        functools.partial(pick_kernel, order),
        jax.ShapeDtypeStruct((own_rows, received), BF16),
        [send_rows, here, ids],
        flops=members * received * own_rows * width,
        scalars=(1,),
    )
    outgoing = call(
        functools.partial(gather_kernel, members, chunks, capacity),
        [chunk_shape] * chunks,
        [latent, pick],
        flops=2 * members * received * own_rows * width,
        limit=40 * 1024 * 1024,
    )
    arrived_first, arrived_last = [
        exchanged([outgoing[order.index(s)] for s in group], group, 1) for group in groups_in
    ]
    query, mult = call(
        functools.partial(query_kernel, order, capacity, head_size),
        [
            jax.ShapeDtypeStruct((per * points, width), BF16),
            jax.ShapeDtypeStruct((received, points), F32),
        ],
        [grid_feat, w_query, neighbours.T, live_count[None, :], here],
        flops=2 * points * width * width,
        scalars=(4,),
    )

    before = len(arrived_first) * capacity
    *parts, w_key_t, w_value_t, place_early, place_late = call(
        functools.partial(
            first_kernel, (members, len(arrived_first), capacity, head_size, 0), [early, late]
        ),
        [
            jax.ShapeDtypeStruct((members, groups, before, per * points), F32),
            jax.ShapeDtypeStruct((members, groups, 1, per * points), F32),
            jax.ShapeDtypeStruct((members, before, width), BF16),
        ]
        + [jax.ShapeDtypeStruct((width, width), BF16)] * 2
        + [jax.ShapeDtypeStruct((own_rows, len(s) * capacity), BF16) for s in (early, late)],
        [query, w_key, w_value, mult, send_rows, here, *arrived_first],
        scratch=[pltpu.VMEM((members, before, width), BF16)],
        flops=4 * members * before * width * width,
        scalars=(5,),
    )
    rows_here = len(arrived_last) * capacity
    predicted, weights, values = call(
        functools.partial(forward_kernel, members, len(arrived_last), capacity, head_size),
        [
            jax.ShapeDtypeStruct((members, variables, points), F32),
            jax.ShapeDtypeStruct((members, groups, received, per * points), BF16),
            jax.ShapeDtypeStruct((members, received, width), BF16),
        ],
        [query, w_key, w_value, w_out, mult, *parts, *arrived_last],
        scratch=[
            pltpu.VMEM((members, rows_here, width), BF16),
            pltpu.VMEM((width, points), BF16),
        ],
        flops=4 * members * rows_here * width * width,
    )
    everyone = [predicted]
    bit = ensembles // 2
    while bit:
        pairs = [(i, i ^ bit) for i in range(ensembles)]
        everyone += [lax.ppermute(p, "member", pairs) for p in everyone]
        bit //= 2
    late_grad = jax.ShapeDtypeStruct(
        (members, groups, len(late) * capacity, per * points), BF16
    )
    *leaving_early, d_scores, late_weights, d_attended = call(
        functools.partial(
            backward_kernel,
            members,
            [order.index(c) for c in early],
            [order.index(c) for c in late],
            capacity,
            head_size,
        ),
        [chunk_shape] * len(early)
        + [late_grad] * 2
        + [jax.ShapeDtypeStruct((members, per * points, width), BF16)],
        [
            query,
            w_key_t,
            w_value_t,
            w_out,
            predicted,
            truth,
            area[None, :],
            var_weight[None, :],
            weights,
            values,
            *everyone[1:],
        ],
        scratch=[pltpu.VMEM((len(early) * step, width), BF16)] * 2,
        flops=4 * members * received * width * width,
    )
    returned_early = exchanged(leaving_early, early, -1)
    leaving_late = call(
        functools.partial(late_rows_kernel, len(late), capacity, head_size),
        [chunk_shape] * len(late),
        [query, w_key_t, w_value_t, d_scores, late_weights, d_attended],
        scratch=[pltpu.VMEM((len(late) * step, width), BF16)] * 2,
        flops=4 * len(late) * step * width * width,
    )
    returned_late = exchanged(leaving_late, late, -1)
    before = call(
        functools.partial(first_sum_kernel, members, capacity),
        jax.ShapeDtypeStruct((members, own_rows, width), F32),
        [place_early, *returned_early],
        flops=2 * len(early) * step * own_rows * width,
    )
    return last_sum(members, capacity, place_late, before, returned_late)


def solution(mesh):
    return jax.shard_map(
        functools.partial(on_device, mesh.shape["grid"], mesh.shape["member"]),
        mesh=mesh,
        in_specs=(
            P("member", "grid", None),
            P("grid", None),
            P(),
            P(),
            P(),
            P(),
            P(None, "grid"),
            P("grid"),
            P(),
            P("grid", None, None),
            P("grid", None),
            P("grid"),
        ),
        out_specs=P("member", "grid", None),
        check_vma=False,
    )
```

```python
import functools
import math

import jax
import jax.numpy as jnp
import numpy as np
from jax import lax
from jax.experimental import pallas as pl
from jax.experimental.pallas import tpu as pltpu
from jax.sharding import PartitionSpec as P

H = 16
LANES = 128
ROOM = 4 * 1024 * 1024
WEIGHT = 40
F32 = jnp.float32
HUGE = float(np.finfo(np.float32).max)
BF16 = jnp.bfloat16
NN = (((1,), (0,)), ((), ()))
NT = (((1,), (1,)), ((), ()))
TN = (((0,), (0,)), ((), ()))
VMEM = pl.BlockSpec(memory_space=pltpu.VMEM)
SMEM = pl.BlockSpec(memory_space=pltpu.SMEM)


def dot(a, b, dims=NN):
    return lax.dot_general(a, b, dims, preferred_element_type=F32)


def call(kernel, out_shape, operands, scratch=(), flops=0, scalars=(), limit=None):
    single = not isinstance(out_shape, (list, tuple))
    outs = [out_shape] if single else out_shape
    moved = sum(x.size * x.dtype.itemsize for x in [*operands, *outs])
    held = sum(math.prod(s.shape) * jnp.dtype(s.dtype).itemsize for s in scratch)
    return pl.pallas_call(
        kernel,
        out_shape=out_shape,
        in_specs=[SMEM if i in scalars else VMEM for i in range(len(operands))],
        out_specs=VMEM if single else [VMEM] * len(outs),
        scratch_shapes=list(scratch),
        compiler_params=pltpu.CompilerParams(vmem_limit_bytes=limit or moved + 2 * held + ROOM),
        cost_estimate=pl.CostEstimate(flops=WEIGHT * flops, bytes_accessed=moved, transcendentals=0),
    )(*operands)


def of_member(block, member, members, chunks, capacity):
    step = members * capacity
    first = member * capacity
    return jnp.concatenate(
        [block[c * step + first : c * step + first + capacity] for c in range(chunks)], axis=0
    )


def by_chunk(blocks, chunks, capacity):
    return jnp.concatenate(
        [b[c * capacity : (c + 1) * capacity] for c in chunks for b in blocks], axis=0
    )


def named_rows(send_ref, me_ref, order):
    return jnp.concatenate(
        [
            send_ref[0, pl.ds(lax.rem(me_ref[0] + shift, send_ref.shape[1]), 1), :]
            for shift in order
        ],
        axis=1,
    )


def one_hot(send_ref, me_ref, order, own_rows):
    rows = named_rows(send_ref, me_ref, order)
    ids = lax.broadcasted_iota(jnp.int32, (own_rows, rows.shape[1]), 0)
    return (rows == ids).astype(F32).astype(BF16)


def ids_kernel(out_ref):
    out_ref[...] = lax.broadcasted_iota(jnp.int32, out_ref.shape, 0)


def pick_kernel(order, send_ref, me_ref, ids_ref, out_ref):
    rows = named_rows(send_ref, me_ref, order)
    out_ref[...] = (rows == ids_ref[...]).astype(F32).astype(BF16)


def one_hot_kernel(orders, send_ref, me_ref, *out_refs):
    for order, out_ref in zip(orders, out_refs):
        out_ref[...] = one_hot(send_ref, me_ref, order, out_ref.shape[0])


def gather_kernel(members, chunks, capacity, latent_ref, pick_ref, *out_refs):
    picked = [dot(pick_ref[...], latent_ref[m], TN) for m in range(members)]
    step = members * capacity
    rows = by_chunk(picked, range(chunks), capacity).astype(BF16)
    for c in range(chunks):
        out_refs[c][...] = rows[c * step : (c + 1) * step]


def query_kernel(
    order, capacity, head_size, feat_ref, w_ref, names_ref, live_ref, me_ref, *out_refs
):
    out_ref, turned_ref, mult_ref = out_refs
    points, width = feat_ref.shape
    slots = names_ref.shape[0]
    per = LANES // head_size
    query = dot(feat_ref[...], w_ref[...]).astype(BF16)
    head = lax.broadcasted_iota(jnp.int32, (points, width), 1) // head_size % per
    for p in range(per):
        out_ref[p * points : (p + 1) * points, :] = jnp.where(
            head == p, query, jnp.zeros_like(query)
        )
    query = query.T
    head = lax.broadcasted_iota(jnp.int32, (width, points), 0) // head_size % per
    for p in range(per):
        turned_ref[:, p * points : (p + 1) * points] = jnp.where(
            head == p, query, jnp.zeros_like(query)
        )
    place = lax.broadcasted_iota(jnp.int32, (capacity, points), 0)
    owners = [lax.rem(me_ref[0] + len(order) - shift, len(order)) for shift in order]
    ids = jnp.concatenate([place + owner * capacity for owner in owners], axis=0)
    mult = jnp.zeros(ids.shape, F32)
    for k in range(slots):
        name = jnp.where(live_ref[...] > k, names_ref[k : k + 1, :], -1)
        mult = mult + jnp.where(ids == name, 1.0, 0.0)
    mult_ref[...] = mult


def project(rows, wk_ref, wv_ref, k_scr, v_ref, offset, members, chunks, capacity, tiles):
    tile = 2 * LANES
    rows_here = pl.ds(offset, chunks * capacity)
    for t in tiles:
        cols = slice(t * tile, (t + 1) * tile)
        keys = dot(rows, wk_ref[:, cols])
        values = dot(rows, wv_ref[:, cols])
        for m in range(members):
            k_scr[m, :, cols] = of_member(keys, m, members, chunks, capacity).astype(BF16)
            v_ref[m, rows_here, cols] = of_member(values, m, members, chunks, capacity).astype(
                BF16
            )


def raised_scores(k_scr, qmt_ref, j, factor, bias, mult):
    members, rows = k_scr.shape[:2]
    cols = slice(j * LANES, (j + 1) * LANES)
    keys = jnp.concatenate([k_scr[m, :, cols] for m in range(members)], axis=0)
    scores = dot(keys, qmt_ref[cols, :])
    both = []
    for m in range(members):
        raised = jnp.exp2(scores[m * rows : (m + 1) * rows] * factor + bias)
        raised = jnp.minimum(mult * raised, HUGE)
        both.append((raised, jnp.sum(raised, axis=0, keepdims=True)))
    return both


def exponent(head_size):
    return head_size ** (-0.5) * math.log2(math.e)


def near_kernel(
    members, chunks, capacity, head_size, before, qmt_ref, wk_ref, wv_ref, mult_ref, *refs
):
    raised_ref, total_ref, v_ref, k_scr = refs[chunks:]
    groups = wk_ref.shape[0] // LANES
    rows = jnp.concatenate([r[...] for r in refs[:chunks]], axis=0)
    tiles = range(wk_ref.shape[0] // (2 * LANES))
    project(rows, wk_ref, wv_ref, k_scr, v_ref, 0, members, chunks, capacity, tiles)
    mult = mult_ref[before : before + k_scr.shape[1], :]
    mult = jnp.concatenate([mult] * (LANES // head_size), axis=1)
    bias = jnp.where(mult > 0.0, 0.0, -jnp.inf)
    for j in range(groups):
        both = raised_scores(k_scr, qmt_ref, j, exponent(head_size), bias, mult)
        for m, (raised, total) in enumerate(both):
            raised_ref[m, j] = raised
            total_ref[m, j] = total


def forward_kernel(
    members,
    chunks,
    capacity,
    head_size,
    qmt_ref,
    wk_ref,
    wv_ref,
    wout_ref,
    mult_ref,
    *refs,
):
    pred_ref, weight_ref, v_ref, k_scr, att_scr = refs[-5:]
    chunk_refs = refs[-5 - chunks : -5]
    parts = refs[: -5 - chunks]
    raised_refs, total_refs, v_refs = parts[0::3], parts[1::3], parts[2::3]
    points = mult_ref.shape[1]
    per = LANES // head_size
    groups = wk_ref.shape[0] // LANES
    done = 0
    for v_part in v_refs:
        v_ref[:, done : done + v_part.shape[1], :] = v_part[...]
        done += v_part.shape[1]
    rows = jnp.concatenate([r[...] for r in chunk_refs], axis=0)
    work = (rows, wk_ref, wv_ref, k_scr, v_ref, done, members, chunks, capacity)
    tiles = groups // 2
    project(*work, [0])
    mult = jnp.concatenate([mult_ref[done:, :]] * per, axis=1)
    bias = jnp.where(mult > 0.0, 0.0, -jnp.inf)
    factor = exponent(head_size)
    for t in range(tiles):
        steps = [(m, j) for j in (2 * t, 2 * t + 1) for m in range(members)]
        ahead = [
            one
            for j in (2 * t, 2 * t + 1)
            for one in raised_scores(k_scr, qmt_ref, j, factor, bias, mult)
        ]
        if t + 1 < tiles:
            project(*work, [t + 1])
        for (m, j), (late, late_total) in zip(steps, ahead):
            raised = jnp.concatenate([r[m, j] for r in raised_refs] + [late], axis=0)
            root = lax.rsqrt(sum([s[m, j] for s in total_refs], late_total))
            weights = (raised * root * root).astype(BF16)
            weight_ref[m, j] = weights
            both = dot(v_ref[m, :, j * LANES : (j + 1) * LANES], weights, TN)
            for p in range(per):
                first = p * head_size
                att_scr[m, pl.ds(j * LANES + first, head_size), :] = both[
                    first : first + head_size, p * points : (p + 1) * points
                ].astype(BF16)
    for m in range(members):
        pred_ref[m] = dot(wout_ref[...], att_scr[m])


def first_kernel(sizes, orders, qmt_ref, wk_ref, wv_ref, mult_ref, send_ref, me_ref, *refs):
    *refs, k_scr = refs
    last = len(refs) - 2 - len(orders)
    wkt_ref, wvt_ref, *place_refs = refs[last:]
    near_kernel(*sizes, qmt_ref, wk_ref, wv_ref, mult_ref, *refs[:last], k_scr)
    wkt_ref[...] = wk_ref[...].T
    wvt_ref[...] = wv_ref[...].T
    one_hot_kernel(orders, send_ref, me_ref, *place_refs)


def return_rows(dk, dv, wkt_ref, wvt_ref, out_refs):
    width = wkt_ref.shape[1]
    tile = 2 * LANES
    step = out_refs[0].shape[0]
    for t in range(width // tile):
        cols = slice(t * tile, (t + 1) * tile)
        rows = dot(dk, wkt_ref[:, cols]) + dot(dv, wvt_ref[:, cols])
        rows = rows.astype(BF16)
        for c, out_ref in enumerate(out_refs):
            out_ref[:, cols] = rows[c * step : (c + 1) * step]


def backward_kernel(
    members,
    chunks,
    capacity,
    head_size,
    qm_ref,
    wkt_ref,
    wvt_ref,
    wout_ref,
    mine_ref,
    truth_ref,
    area_ref,
    var_ref,
    weight_ref,
    v_ref,
    *refs,
):
    other_refs = refs[: len(refs) - chunks - 6]
    out_refs = refs[len(other_refs) : -6]
    ds_ref, da_ref, dk_scr, dv_scr, sum_scr, dat_scr = refs[-6:]
    now = chunks * capacity
    width = wkt_ref.shape[1]
    points = truth_ref.shape[1]
    every_refs = (mine_ref, *other_refs)
    total = sum(r.shape[0] for r in every_refs)
    per = LANES // head_size
    groups = width // LANES
    scale = head_size ** (-0.5)
    variables = var_ref.shape[1]
    wide = -variables % LANES
    var = jnp.concatenate([var_ref[...], jnp.zeros((1, wide), F32)], axis=1)
    var = jnp.broadcast_to(var, (LANES, variables + wide)).T[:variables, :1]
    factor = area_ref[...] * var
    head = lax.broadcasted_iota(jnp.int32, (points, 2 * LANES), 1) // head_size % per
    turned = lax.broadcasted_iota(jnp.int32, (2 * LANES, points), 0) // head_size % per
    dpreds = []
    for m in range(members):
        mine = mine_ref[m]
        miss = mine - truth_ref[...]
        first = miss * lax.rsqrt(1.0 + miss * miss) / total
        second = jnp.zeros_like(mine)
        for every_ref in every_refs:
            for f in range(every_ref.shape[0]):
                paired = mine - every_ref[f]
                second = second + paired * lax.rsqrt(1.0 + paired * paired)
        dpred = (factor * (first - second / (total * (total - 1)))).astype(BF16)
        dpreds.append(dpred)
    tile = 2 * LANES
    tiles = width // tile

    def attended_grad(t):
        cols = slice(t * tile, (t + 1) * tile)
        for m in range(members):
            grad = dot(dpreds[m], wout_ref[:, cols], TN).astype(BF16)
            for p in range(per):
                da_ref[m, p * points : (p + 1) * points, cols] = jnp.where(
                    head == p, grad, jnp.zeros_like(grad)
                )
            grad = dot(wout_ref[:, cols], dpreds[m], TN).astype(BF16)
            for p in range(per):
                dat_scr[m, cols, p * points : (p + 1) * points] = jnp.where(
                    turned == p, grad, jnp.zeros_like(grad)
                )

    def probs_grad(m, j):
        cols = slice(j * LANES, (j + 1) * LANES)
        return dot(v_ref[m, :, cols], dat_scr[m, cols, :])

    attended_grad(0)
    for t in range(tiles):
        steps = [(j, m) for j in (2 * t, 2 * t + 1) for m in range(members)]
        ahead = [probs_grad(m, j) for j, m in steps]
        if t + 1 < tiles:
            attended_grad(t + 1)
        if t > 0:
            before = slice((t - 1) * tile, t * tile)
            more = dot(dk_scr[:, before], wkt_ref[before, :])
            more = more + dot(dv_scr[:, before], wvt_ref[before, :])
            sum_scr[...] = more if t == 1 else sum_scr[...] + more
        d_keys, d_values = [], []
        for (j, m), d_probs in zip(steps, ahead):
            cols = slice(j * LANES, (j + 1) * LANES)
            weights = weight_ref[m, j].astype(F32)
            inner = jnp.sum(weights * d_probs, axis=0, keepdims=True)
            d_scores = (weights * (d_probs - inner)).astype(BF16)
            ds_ref[m, j] = d_scores[now:]
            d_keys.append(d_scores[:now])
            d_values.append(dot(weight_ref[m, j, :now, :], da_ref[m, :, cols]))
            if m == members - 1:
                both = dot(jnp.concatenate(d_keys, axis=0), qm_ref[:, cols]) * scale
                d_keys = [both[i * now : (i + 1) * now] for i in range(members)]
                dk_scr[:, cols] = by_chunk(d_keys, range(chunks), capacity).astype(BF16)
                dv_scr[:, cols] = by_chunk(d_values, range(chunks), capacity).astype(BF16)
                d_keys, d_values = [], []
    last = slice((tiles - 1) * tile, width)
    step = out_refs[0].shape[0]
    for t in range(tiles):
        cols = slice(t * tile, (t + 1) * tile)
        rows = dot(dk_scr[:, last], wkt_ref[last, cols])
        rows = rows + dot(dv_scr[:, last], wvt_ref[last, cols])
        if tiles > 1:
            rows = rows + sum_scr[:, cols]
        rows = rows.astype(BF16)
        for c, out_ref in enumerate(out_refs):
            out_ref[:, cols] = rows[c * step : (c + 1) * step]


def late_rows_kernel(
    chunks, capacity, head_size, qm_ref, wkt_ref, wvt_ref, ds_ref, w_ref, da_ref, *refs
):
    out_refs = refs[:chunks]
    dk_scr, dv_scr = refs[chunks:]
    members, groups, rows = ds_ref.shape[:3]
    done = w_ref.shape[2] - rows
    scale = head_size ** (-0.5)
    for j in range(groups):
        cols = slice(j * LANES, (j + 1) * LANES)
        both = jnp.concatenate([ds_ref[m, j] for m in range(members)], axis=0)
        both = dot(both, qm_ref[:, cols]) * scale
        d_keys = [both[m * rows : (m + 1) * rows] for m in range(members)]
        d_values = [dot(w_ref[m, j, done:, :], da_ref[m, :, cols]) for m in range(members)]
        dk_scr[:, cols] = by_chunk(d_keys, range(chunks), capacity).astype(BF16)
        dv_scr[:, cols] = by_chunk(d_values, range(chunks), capacity).astype(BF16)
    return_rows(dk_scr[...], dv_scr[...], wkt_ref, wvt_ref, out_refs)


def first_sum_kernel(members, capacity, place_ref, *refs):
    *_, out_ref = refs
    chunks = len(refs) - 1
    place = place_ref[...]
    back = jnp.concatenate([r[...] for r in refs[:chunks]], axis=0).astype(F32)
    for m in range(members):
        mine = of_member(back, m, members, chunks, capacity).astype(BF16)
        out_ref[m] = dot(place, mine)


def last_sum_kernel(members, capacity, place_ref, before_ref, *refs):
    chunks = len(refs) - 3
    out_ref, sum_scr, sems = refs[chunks:]
    parts = sems.shape[1]
    part = out_ref.shape[1] // parts
    back = jnp.concatenate([r[...] for r in refs[:chunks]], axis=0).astype(F32)
    mine = [
        of_member(back, m, members, chunks, capacity).astype(BF16) for m in range(members)
    ]
    sends = []
    for m in range(members):
        for p in range(parts):
            rows = slice(p * part, (p + 1) * part)
            sum_scr[m, rows, :] = before_ref[m, rows, :] + dot(place_ref[rows, :], mine[m])
            there = pl.ds(p * part, part)
            send = pltpu.make_async_copy(
                sum_scr.at[m, there], out_ref.at[m, there], sems.at[m, p]
            )
            send.start()
            sends.append(send)
    for send in sends:
        send.wait()


def last_sum(members, capacity, place, before, blocks):
    step, width = blocks[0].shape
    own_rows = before.shape[1]
    parts = next(p for p in (5, 4, 2, 1) if own_rows % (p * 16) == 0)
    moved = len(blocks) * step * width * 2 + 2 * members * own_rows * width * 4
    return pl.pallas_call(
        functools.partial(last_sum_kernel, members, capacity),
        out_shape=jax.ShapeDtypeStruct((members, own_rows, width), F32),
        in_specs=[VMEM] * (2 + len(blocks)),
        out_specs=pl.BlockSpec(memory_space=pltpu.HBM),
        scratch_shapes=[
            pltpu.VMEM((members, own_rows, width), F32),
            pltpu.SemaphoreType.DMA((members, parts)),
        ],
        compiler_params=pltpu.CompilerParams(vmem_limit_bytes=2 * moved + 2 * ROOM),
        cost_estimate=pl.CostEstimate(
            flops=2 * len(blocks) * step * own_rows * width,
            bytes_accessed=moved,
            transcendentals=0,
        ),
    )(place, before, *blocks)


def shifts_from(chunks, first):
    return tuple(dict.fromkeys([0, *(s % chunks for s in first), *range(chunks)]))


def on_device(
    chunks,
    ensembles,
    latent,
    grid_feat,
    w_query,
    w_key,
    w_value,
    w_out,
    truth,
    area,
    var_weight,
    send_rows,
    neighbours,
    live_count,
):
    members, own_rows, width = latent.shape
    points, slots = neighbours.shape
    variables = w_out.shape[0]
    capacity = send_rows.shape[2]
    head_size = width // H
    per = LANES // head_size
    groups = width // LANES
    step = members * capacity
    received = chunks * capacity
    me = lax.axis_index("grid")
    half = chunks // 2
    order = shifts_from(chunks, (half, 1, -1, half - 1, half + 1, 2, -2))
    early, late = order[:half], order[half:]
    here = me[None]

    def exchanged(blocks, shifts, sign):
        return [
            b
            if s == 0
            else lax.ppermute(b, "grid", [(i, (i + sign * s) % chunks) for i in range(chunks)])
            for s, b in zip(shifts, blocks)
        ]

    chunk_shape = jax.ShapeDtypeStruct((step, width), BF16)
    ids = call(
        ids_kernel,
        jax.ShapeDtypeStruct((own_rows, received), jnp.int32),
        [],
        flops=members * received * own_rows * width,
    )
    pick = call(
        functools.partial(pick_kernel, order),
        jax.ShapeDtypeStruct((own_rows, received), BF16),
        [send_rows, here, ids],
        scalars=(1,),
    )
    outgoing = call(
        functools.partial(gather_kernel, members, chunks, capacity),
        [chunk_shape] * chunks,
        [latent, pick],
        flops=2 * members * received * own_rows * width,
        limit=40 * 1024 * 1024,
    )
    arrived_first, arrived_last = [
        exchanged([outgoing[order.index(s)] for s in group], group, 1) for group in (early, late)
    ]
    query, query_t, mult = call(
        functools.partial(query_kernel, order, capacity, head_size),
        [
            jax.ShapeDtypeStruct((per * points, width), BF16),
            jax.ShapeDtypeStruct((width, per * points), BF16),
            jax.ShapeDtypeStruct((received, points), F32),
        ],
        [grid_feat, w_query, neighbours.T, live_count[None, :], here],
        flops=2 * points * width * width,
        scalars=(4,),
    )

    before = len(arrived_first) * capacity
    *parts, w_key_t, w_value_t, place_early, place_late = call(
        functools.partial(
            first_kernel, (members, len(arrived_first), capacity, head_size, 0), [early, late]
        ),
        [
            jax.ShapeDtypeStruct((members, groups, before, per * points), F32),
            jax.ShapeDtypeStruct((members, groups, 1, per * points), F32),
            jax.ShapeDtypeStruct((members, before, width), BF16),
        ]
        + [jax.ShapeDtypeStruct((width, width), BF16)] * 2
        + [jax.ShapeDtypeStruct((own_rows, len(s) * capacity), BF16) for s in (early, late)],
        [query_t, w_key, w_value, mult, send_rows, here, *arrived_first],
        scratch=[pltpu.VMEM((members, before, width), BF16)],
        flops=4 * members * before * width * width,
        scalars=(5,),
    )
    rows_here = len(arrived_last) * capacity
    predicted, weights, values = call(
        functools.partial(forward_kernel, members, len(arrived_last), capacity, head_size),
        [
            jax.ShapeDtypeStruct((members, variables, points), F32),
            jax.ShapeDtypeStruct((members, groups, received, per * points), BF16),
            jax.ShapeDtypeStruct((members, received, width), BF16),
        ],
        [query_t, w_key, w_value, w_out, mult, *parts, *arrived_last],
        scratch=[
            pltpu.VMEM((members, rows_here, width), BF16),
            pltpu.VMEM((members, width, points), BF16),
        ],
        flops=4 * members * rows_here * width * width,
    )
    everyone = [predicted]
    bit = ensembles // 2
    while bit:
        pairs = [(i, i ^ bit) for i in range(ensembles)]
        everyone += [lax.ppermute(p, "member", pairs) for p in everyone]
        bit //= 2
    late_grad = jax.ShapeDtypeStruct(
        (members, groups, len(late) * capacity, per * points), BF16
    )
    *leaving_early, d_scores, d_attended = call(
        functools.partial(backward_kernel, members, len(early), capacity, head_size),
        [chunk_shape] * len(early)
        + [late_grad, jax.ShapeDtypeStruct((members, per * points, width), BF16)],
        [
            query,
            w_key_t,
            w_value_t,
            w_out,
            predicted,
            truth,
            area[None, :],
            var_weight[None, :],
            weights,
            values,
            *everyone[1:],
        ],
        scratch=[pltpu.VMEM((len(early) * step, width), BF16)] * 2
        + [
            pltpu.VMEM((len(early) * step, width), F32),
            pltpu.VMEM((members, width, per * points), BF16),
        ],
        flops=4 * members * received * width * width,
    )
    returned_early = exchanged(leaving_early, early, -1)
    leaving_late = call(
        functools.partial(late_rows_kernel, len(late), capacity, head_size),
        [chunk_shape] * len(late),
        [query, w_key_t, w_value_t, d_scores, weights, d_attended],
        scratch=[pltpu.VMEM((len(late) * step, width), BF16)] * 2,
        flops=4 * len(late) * step * width * width,
    )
    returned_late = exchanged(leaving_late, late, -1)
    before = call(
        functools.partial(first_sum_kernel, members, capacity),
        jax.ShapeDtypeStruct((members, own_rows, width), F32),
        [place_early, *returned_early],
        flops=2 * len(early) * step * own_rows * width,
    )
    return last_sum(members, capacity, place_late, before, returned_late)


def solution(mesh):
    return jax.shard_map(
        functools.partial(on_device, mesh.shape["grid"], mesh.shape["member"]),
        mesh=mesh,
        in_specs=(
            P("member", "grid", None),
            P("grid", None),
            P(),
            P(),
            P(),
            P(),
            P(None, "grid"),
            P("grid"),
            P(),
            P("grid", None, None),
            P("grid", None),
            P("grid"),
        ),
        out_specs=P("member", "grid", None),
        check_vma=False,
    )
```

```python
import functools
import math

import jax
import jax.numpy as jnp
import numpy as np
from jax import lax
from jax.experimental import pallas as pl
from jax.experimental.pallas import tpu as pltpu
from jax.sharding import PartitionSpec as P

H = 16
LANES = 128
ROOM = 4 * 1024 * 1024
WEIGHT = 40
F32 = jnp.float32
HUGE = float(np.finfo(np.float32).max)
BF16 = jnp.bfloat16
NN = (((1,), (0,)), ((), ()))
NT = (((1,), (1,)), ((), ()))
TN = (((0,), (0,)), ((), ()))
VMEM = pl.BlockSpec(memory_space=pltpu.VMEM)
SMEM = pl.BlockSpec(memory_space=pltpu.SMEM)


def dot(a, b, dims=NN):
    return lax.dot_general(a, b, dims, preferred_element_type=F32)


def call(kernel, out_shape, operands, scratch=(), flops=0, scalars=(), limit=None):
    single = not isinstance(out_shape, (list, tuple))
    outs = [out_shape] if single else out_shape
    moved = sum(x.size * x.dtype.itemsize for x in [*operands, *outs])
    held = sum(math.prod(s.shape) * jnp.dtype(s.dtype).itemsize for s in scratch)
    return pl.pallas_call(
        kernel,
        out_shape=out_shape,
        in_specs=[SMEM if i in scalars else VMEM for i in range(len(operands))],
        out_specs=VMEM if single else [VMEM] * len(outs),
        scratch_shapes=list(scratch),
        compiler_params=pltpu.CompilerParams(vmem_limit_bytes=limit or moved + 2 * held + ROOM),
        cost_estimate=pl.CostEstimate(flops=WEIGHT * flops, bytes_accessed=moved, transcendentals=0),
    )(*operands)


def of_member(block, member, members, chunks, capacity):
    step = members * capacity
    first = member * capacity
    return jnp.concatenate(
        [block[c * step + first : c * step + first + capacity] for c in range(chunks)], axis=0
    )


def by_chunk(blocks, chunks, capacity):
    return jnp.concatenate(
        [b[c * capacity : (c + 1) * capacity] for c in chunks for b in blocks], axis=0
    )


def named_rows(send_ref, me_ref, order):
    return jnp.concatenate(
        [
            send_ref[0, pl.ds(lax.rem(me_ref[0] + shift, send_ref.shape[1]), 1), :]
            for shift in order
        ],
        axis=1,
    )


def one_hot(send_ref, me_ref, order, own_rows):
    rows = named_rows(send_ref, me_ref, order)
    ids = lax.broadcasted_iota(jnp.int32, (own_rows, rows.shape[1]), 0)
    return (rows == ids).astype(F32).astype(BF16)


def ids_kernel(out_ref):
    out_ref[...] = lax.broadcasted_iota(jnp.int32, out_ref.shape, 0)


def pick_kernel(order, send_ref, me_ref, ids_ref, out_ref):
    rows = named_rows(send_ref, me_ref, order)
    out_ref[...] = (rows == ids_ref[...]).astype(F32).astype(BF16)


def one_hot_kernel(orders, send_ref, me_ref, *out_refs):
    for order, out_ref in zip(orders, out_refs):
        out_ref[...] = one_hot(send_ref, me_ref, order, out_ref.shape[0])


def gather_kernel(members, chunks, capacity, latent_ref, pick_ref, *out_refs):
    picked = [dot(pick_ref[...], latent_ref[m], TN) for m in range(members)]
    step = members * capacity
    rows = by_chunk(picked, range(chunks), capacity).astype(BF16)
    for c in range(chunks):
        out_refs[c][...] = rows[c * step : (c + 1) * step]


def query_kernel(
    order, capacity, head_size, feat_ref, w_ref, names_ref, live_ref, me_ref, *out_refs
):
    out_ref, turned_ref, mult_ref = out_refs
    points, width = feat_ref.shape
    slots = names_ref.shape[0]
    per = LANES // head_size
    query = dot(feat_ref[...], w_ref[...]).astype(BF16)
    head = lax.broadcasted_iota(jnp.int32, (points, width), 1) // head_size % per
    for p in range(per):
        out_ref[p * points : (p + 1) * points, :] = jnp.where(
            head == p, query, jnp.zeros_like(query)
        )
    query = query.T
    head = lax.broadcasted_iota(jnp.int32, (width, points), 0) // head_size % per
    for p in range(per):
        turned_ref[:, p * points : (p + 1) * points] = jnp.where(
            head == p, query, jnp.zeros_like(query)
        )
    place = lax.broadcasted_iota(jnp.int32, (capacity, points), 0)
    owners = [lax.rem(me_ref[0] + len(order) - shift, len(order)) for shift in order]
    ids = jnp.concatenate([place + owner * capacity for owner in owners], axis=0)
    mult = jnp.zeros(ids.shape, F32)
    for k in range(slots):
        name = jnp.where(live_ref[...] > k, names_ref[k : k + 1, :], -1)
        mult = mult + jnp.where(ids == name, 1.0, 0.0)
    mult_ref[...] = mult


def project(rows, wk_ref, wv_ref, k_scr, v_ref, offset, members, chunks, capacity, tiles):
    tile = 2 * LANES
    rows_here = pl.ds(offset, chunks * capacity)
    for t in tiles:
        cols = slice(t * tile, (t + 1) * tile)
        keys = dot(rows, wk_ref[:, cols])
        values = dot(rows, wv_ref[:, cols])
        for m in range(members):
            k_scr[m, :, cols] = of_member(keys, m, members, chunks, capacity).astype(BF16)
            v_ref[m, rows_here, cols] = of_member(values, m, members, chunks, capacity).astype(
                BF16
            )


def raised_scores(k_scr, qmt_ref, j, factor, bias, mult):
    members, rows = k_scr.shape[:2]
    cols = slice(j * LANES, (j + 1) * LANES)
    keys = jnp.concatenate([k_scr[m, :, cols] for m in range(members)], axis=0)
    scores = dot(keys, qmt_ref[cols, :])
    both = []
    for m in range(members):
        raised = jnp.exp2(scores[m * rows : (m + 1) * rows] * factor + bias)
        raised = jnp.minimum(mult * raised, HUGE)
        both.append((raised, jnp.sum(raised, axis=0, keepdims=True)))
    return both


def exponent(head_size):
    return head_size ** (-0.5) * math.log2(math.e)


def near_kernel(
    members, chunks, capacity, head_size, before, qmt_ref, wk_ref, wv_ref, mult_ref, *refs
):
    raised_ref, total_ref, v_ref, k_scr = refs[chunks:]
    groups = wk_ref.shape[0] // LANES
    rows = jnp.concatenate([r[...] for r in refs[:chunks]], axis=0)
    tiles = range(wk_ref.shape[0] // (2 * LANES))
    project(rows, wk_ref, wv_ref, k_scr, v_ref, 0, members, chunks, capacity, tiles)
    mult = mult_ref[before : before + k_scr.shape[1], :]
    mult = jnp.concatenate([mult] * (LANES // head_size), axis=1)
    bias = jnp.where(mult > 0.0, 0.0, -jnp.inf)
    for j in range(groups):
        both = raised_scores(k_scr, qmt_ref, j, exponent(head_size), bias, mult)
        for m, (raised, total) in enumerate(both):
            raised_ref[m, j] = raised
            total_ref[m, j] = total


def forward_kernel(
    members,
    chunks,
    capacity,
    head_size,
    qmt_ref,
    wk_ref,
    wv_ref,
    wout_ref,
    mult_ref,
    *refs,
):
    pred_ref, weight_ref, v_ref, k_scr, att_scr = refs[-5:]
    chunk_refs = refs[-5 - chunks : -5]
    parts = refs[: -5 - chunks]
    raised_refs, total_refs, v_refs = parts[0::3], parts[1::3], parts[2::3]
    points = mult_ref.shape[1]
    per = LANES // head_size
    groups = wk_ref.shape[0] // LANES
    done = 0
    for v_part in v_refs:
        v_ref[:, done : done + v_part.shape[1], :] = v_part[...]
        done += v_part.shape[1]
    rows = jnp.concatenate([r[...] for r in chunk_refs], axis=0)
    work = (rows, wk_ref, wv_ref, k_scr, v_ref, done, members, chunks, capacity)
    tiles = groups // 2
    project(*work, [0])
    mult = jnp.concatenate([mult_ref[done:, :]] * per, axis=1)
    bias = jnp.where(mult > 0.0, 0.0, -jnp.inf)
    factor = exponent(head_size)
    for t in range(tiles):
        steps = [(m, j) for j in (2 * t, 2 * t + 1) for m in range(members)]
        ahead = [
            one
            for j in (2 * t, 2 * t + 1)
            for one in raised_scores(k_scr, qmt_ref, j, factor, bias, mult)
        ]
        if t + 1 < tiles:
            project(*work, [t + 1])
        for (m, j), (late, late_total) in zip(steps, ahead):
            raised = jnp.concatenate([r[m, j] for r in raised_refs] + [late], axis=0)
            root = lax.rsqrt(sum([s[m, j] for s in total_refs], late_total))
            weights = (raised * root * root).astype(BF16)
            weight_ref[m, j] = weights
            both = dot(v_ref[m, :, j * LANES : (j + 1) * LANES], weights, TN)
            for p in range(per):
                first = p * head_size
                att_scr[m, pl.ds(j * LANES + first, head_size), :] = both[
                    first : first + head_size, p * points : (p + 1) * points
                ].astype(BF16)
    for m in range(members):
        pred_ref[m] = dot(wout_ref[...], att_scr[m])


def first_kernel(sizes, orders, qmt_ref, wk_ref, wv_ref, mult_ref, send_ref, me_ref, *refs):
    *refs, k_scr = refs
    last = len(refs) - 2 - len(orders)
    wkt_ref, wvt_ref, *place_refs = refs[last:]
    near_kernel(*sizes, qmt_ref, wk_ref, wv_ref, mult_ref, *refs[:last], k_scr)
    wkt_ref[...] = wk_ref[...].T
    wvt_ref[...] = wv_ref[...].T
    one_hot_kernel(orders, send_ref, me_ref, *place_refs)


def return_rows(dk, dv, wkt_ref, wvt_ref, out_refs):
    width = wkt_ref.shape[1]
    tile = 2 * LANES
    step = out_refs[0].shape[0]
    for t in range(width // tile):
        cols = slice(t * tile, (t + 1) * tile)
        rows = dot(dk, wkt_ref[:, cols]) + dot(dv, wvt_ref[:, cols])
        rows = rows.astype(BF16)
        for c, out_ref in enumerate(out_refs):
            out_ref[:, cols] = rows[c * step : (c + 1) * step]


def pair_terms(mine, other_refs):
    total = jnp.zeros_like(mine)
    for other_ref in other_refs:
        for f in range(other_ref.shape[0]):
            paired = mine - other_ref[f]
            total = total + paired * lax.rsqrt(1.0 + paired * paired)
    return total


def score_kernel(ensemble, mine_ref, truth_ref, area_ref, var_ref, *refs):
    *other_refs, base_ref, factor_ref = refs
    variables = var_ref.shape[1]
    wide = -variables % LANES
    var = jnp.concatenate([var_ref[...], jnp.zeros((1, wide), F32)], axis=1)
    var = jnp.broadcast_to(var, (LANES, variables + wide)).T[:variables, :1]
    factor_ref[...] = area_ref[...] * var
    for m in range(mine_ref.shape[0]):
        mine = mine_ref[m]
        miss = mine - truth_ref[...]
        first = miss * lax.rsqrt(1.0 + miss * miss) / ensemble
        second = pair_terms(mine, [mine_ref, *other_refs]) / (ensemble * (ensemble - 1))
        base_ref[m] = first - second


def backward_kernel(
    members,
    ensemble,
    chunks,
    capacity,
    head_size,
    qm_ref,
    wkt_ref,
    wvt_ref,
    wout_ref,
    mine_ref,
    base_ref,
    factor_ref,
    weight_ref,
    v_ref,
    *refs,
):
    other_refs = refs[: len(refs) - chunks - 6]
    out_refs = refs[len(other_refs) : -6]
    ds_ref, da_ref, dk_scr, dv_scr, sum_scr, dat_scr = refs[-6:]
    now = chunks * capacity
    width = wkt_ref.shape[1]
    points = base_ref.shape[2]
    per = LANES // head_size
    groups = width // LANES
    scale = head_size ** (-0.5)
    head = lax.broadcasted_iota(jnp.int32, (points, 2 * LANES), 1) // head_size % per
    turned = lax.broadcasted_iota(jnp.int32, (2 * LANES, points), 0) // head_size % per
    dpreds = []
    for m in range(members):
        mine = mine_ref[m]
        more = pair_terms(mine, other_refs) / (ensemble * (ensemble - 1))
        dpred = (factor_ref[...] * (base_ref[m] - more)).astype(BF16)
        dpreds.append(dpred)
    tile = 2 * LANES
    tiles = width // tile

    def attended_grad(t):
        cols = slice(t * tile, (t + 1) * tile)
        for m in range(members):
            grad = dot(dpreds[m], wout_ref[:, cols], TN).astype(BF16)
            for p in range(per):
                da_ref[m, p * points : (p + 1) * points, cols] = jnp.where(
                    head == p, grad, jnp.zeros_like(grad)
                )
            grad = dot(wout_ref[:, cols], dpreds[m], TN).astype(BF16)
            for p in range(per):
                dat_scr[m, cols, p * points : (p + 1) * points] = jnp.where(
                    turned == p, grad, jnp.zeros_like(grad)
                )

    def probs_grad(m, j):
        cols = slice(j * LANES, (j + 1) * LANES)
        return dot(v_ref[m, :, cols], dat_scr[m, cols, :])

    attended_grad(0)
    for t in range(tiles):
        steps = [(j, m) for j in (2 * t, 2 * t + 1) for m in range(members)]
        ahead = [probs_grad(m, j) for j, m in steps]
        if t + 1 < tiles:
            attended_grad(t + 1)
        if t > 0:
            before = slice((t - 1) * tile, t * tile)
            more = dot(dk_scr[:, before], wkt_ref[before, :])
            more = more + dot(dv_scr[:, before], wvt_ref[before, :])
            sum_scr[...] = more if t == 1 else sum_scr[...] + more
        d_keys, d_values = [], []
        for (j, m), d_probs in zip(steps, ahead):
            cols = slice(j * LANES, (j + 1) * LANES)
            weights = weight_ref[m, j].astype(F32)
            inner = jnp.sum(weights * d_probs, axis=0, keepdims=True)
            d_scores = (weights * (d_probs - inner)).astype(BF16)
            ds_ref[m, j] = d_scores[now:]
            d_keys.append(d_scores[:now])
            d_values.append(dot(weight_ref[m, j, :now, :], da_ref[m, :, cols]))
            if m == members - 1:
                both = dot(jnp.concatenate(d_keys, axis=0), qm_ref[:, cols]) * scale
                d_keys = [both[i * now : (i + 1) * now] for i in range(members)]
                dk_scr[:, cols] = by_chunk(d_keys, range(chunks), capacity).astype(BF16)
                dv_scr[:, cols] = by_chunk(d_values, range(chunks), capacity).astype(BF16)
                d_keys, d_values = [], []
    last = slice((tiles - 1) * tile, width)
    step = out_refs[0].shape[0]
    for t in range(tiles):
        cols = slice(t * tile, (t + 1) * tile)
        rows = dot(dk_scr[:, last], wkt_ref[last, cols])
        rows = rows + dot(dv_scr[:, last], wvt_ref[last, cols])
        if tiles > 1:
            rows = rows + sum_scr[:, cols]
        rows = rows.astype(BF16)
        for c, out_ref in enumerate(out_refs):
            out_ref[:, cols] = rows[c * step : (c + 1) * step]


def late_rows_kernel(
    chunks, capacity, head_size, qm_ref, wkt_ref, wvt_ref, ds_ref, w_ref, da_ref, *refs
):
    out_refs = refs[:chunks]
    dk_scr, dv_scr = refs[chunks:]
    members, groups, rows = ds_ref.shape[:3]
    done = w_ref.shape[2] - rows
    scale = head_size ** (-0.5)
    for j in range(groups):
        cols = slice(j * LANES, (j + 1) * LANES)
        both = jnp.concatenate([ds_ref[m, j] for m in range(members)], axis=0)
        both = dot(both, qm_ref[:, cols]) * scale
        d_keys = [both[m * rows : (m + 1) * rows] for m in range(members)]
        d_values = [dot(w_ref[m, j, done:, :], da_ref[m, :, cols]) for m in range(members)]
        dk_scr[:, cols] = by_chunk(d_keys, range(chunks), capacity).astype(BF16)
        dv_scr[:, cols] = by_chunk(d_values, range(chunks), capacity).astype(BF16)
    return_rows(dk_scr[...], dv_scr[...], wkt_ref, wvt_ref, out_refs)


def first_sum_kernel(members, capacity, place_ref, *refs):
    *_, out_ref = refs
    chunks = len(refs) - 1
    place = place_ref[...]
    back = jnp.concatenate([r[...] for r in refs[:chunks]], axis=0).astype(F32)
    for m in range(members):
        mine = of_member(back, m, members, chunks, capacity).astype(BF16)
        out_ref[m] = dot(place, mine)


def last_sum_kernel(members, capacity, place_ref, before_ref, *refs):
    chunks = len(refs) - 3
    out_ref, sum_scr, sems = refs[chunks:]
    parts = sems.shape[1]
    part = out_ref.shape[1] // parts
    back = jnp.concatenate([r[...] for r in refs[:chunks]], axis=0).astype(F32)
    mine = [
        of_member(back, m, members, chunks, capacity).astype(BF16) for m in range(members)
    ]
    sends = []
    for m in range(members):
        for p in range(parts):
            rows = slice(p * part, (p + 1) * part)
            sum_scr[m, rows, :] = before_ref[m, rows, :] + dot(place_ref[rows, :], mine[m])
            there = pl.ds(p * part, part)
            send = pltpu.make_async_copy(
                sum_scr.at[m, there], out_ref.at[m, there], sems.at[m, p]
            )
            send.start()
            sends.append(send)
    for send in sends:
        send.wait()


def last_sum(members, capacity, place, before, blocks):
    step, width = blocks[0].shape
    own_rows = before.shape[1]
    parts = next(p for p in (5, 4, 2, 1) if own_rows % (p * 16) == 0)
    moved = len(blocks) * step * width * 2 + 2 * members * own_rows * width * 4
    return pl.pallas_call(
        functools.partial(last_sum_kernel, members, capacity),
        out_shape=jax.ShapeDtypeStruct((members, own_rows, width), F32),
        in_specs=[VMEM] * (2 + len(blocks)),
        out_specs=pl.BlockSpec(memory_space=pltpu.HBM),
        scratch_shapes=[
            pltpu.VMEM((members, own_rows, width), F32),
            pltpu.SemaphoreType.DMA((members, parts)),
        ],
        compiler_params=pltpu.CompilerParams(vmem_limit_bytes=2 * moved + 2 * ROOM),
        cost_estimate=pl.CostEstimate(
            flops=2 * len(blocks) * step * own_rows * width,
            bytes_accessed=moved,
            transcendentals=0,
        ),
    )(place, before, *blocks)


def shifts_from(chunks, first):
    return tuple(dict.fromkeys([0, *(s % chunks for s in first), *range(chunks)]))


def on_device(
    chunks,
    ensembles,
    latent,
    grid_feat,
    w_query,
    w_key,
    w_value,
    w_out,
    truth,
    area,
    var_weight,
    send_rows,
    neighbours,
    live_count,
):
    members, own_rows, width = latent.shape
    points, slots = neighbours.shape
    variables = w_out.shape[0]
    capacity = send_rows.shape[2]
    head_size = width // H
    per = LANES // head_size
    groups = width // LANES
    step = members * capacity
    received = chunks * capacity
    me = lax.axis_index("grid")
    half = chunks // 2
    order = shifts_from(chunks, (half, 1, -1, half - 1, half + 1, 2, -2))
    early, late = order[:half], order[half:]
    here = me[None]

    def exchanged(blocks, shifts, sign):
        return [
            b
            if s == 0
            else lax.ppermute(b, "grid", [(i, (i + sign * s) % chunks) for i in range(chunks)])
            for s, b in zip(shifts, blocks)
        ]

    chunk_shape = jax.ShapeDtypeStruct((step, width), BF16)
    ids = call(
        ids_kernel,
        jax.ShapeDtypeStruct((own_rows, received), jnp.int32),
        [],
        flops=members * received * own_rows * width,
    )
    pick = call(
        functools.partial(pick_kernel, order),
        jax.ShapeDtypeStruct((own_rows, received), BF16),
        [send_rows, here, ids],
        scalars=(1,),
    )
    outgoing = call(
        functools.partial(gather_kernel, members, chunks, capacity),
        [chunk_shape] * chunks,
        [latent, pick],
        flops=2 * members * received * own_rows * width,
        limit=40 * 1024 * 1024,
    )
    arrived_first, arrived_last = [
        exchanged([outgoing[order.index(s)] for s in group], group, 1) for group in (early, late)
    ]
    query, query_t, mult = call(
        functools.partial(query_kernel, order, capacity, head_size),
        [
            jax.ShapeDtypeStruct((per * points, width), BF16),
            jax.ShapeDtypeStruct((width, per * points), BF16),
            jax.ShapeDtypeStruct((received, points), F32),
        ],
        [grid_feat, w_query, neighbours.T, live_count[None, :], here],
        flops=2 * points * width * width,
        scalars=(4,),
    )

    before = len(arrived_first) * capacity
    *parts, w_key_t, w_value_t, place_early, place_late = call(
        functools.partial(
            first_kernel, (members, len(arrived_first), capacity, head_size, 0), [early, late]
        ),
        [
            jax.ShapeDtypeStruct((members, groups, before, per * points), F32),
            jax.ShapeDtypeStruct((members, groups, 1, per * points), F32),
            jax.ShapeDtypeStruct((members, before, width), BF16),
        ]
        + [jax.ShapeDtypeStruct((width, width), BF16)] * 2
        + [jax.ShapeDtypeStruct((own_rows, len(s) * capacity), BF16) for s in (early, late)],
        [query_t, w_key, w_value, mult, send_rows, here, *arrived_first],
        scratch=[pltpu.VMEM((members, before, width), BF16)],
        flops=4 * members * before * width * width,
        scalars=(5,),
    )
    rows_here = len(arrived_last) * capacity
    predicted, weights, values = call(
        functools.partial(forward_kernel, members, len(arrived_last), capacity, head_size),
        [
            jax.ShapeDtypeStruct((members, variables, points), F32),
            jax.ShapeDtypeStruct((members, groups, received, per * points), BF16),
            jax.ShapeDtypeStruct((members, received, width), BF16),
        ],
        [query_t, w_key, w_value, w_out, mult, *parts, *arrived_last],
        scratch=[
            pltpu.VMEM((members, rows_here, width), BF16),
            pltpu.VMEM((members, width, points), BF16),
        ],
        flops=4 * members * rows_here * width * width,
    )
    everyone = [predicted]
    bit = ensembles // 2
    while bit:
        pairs = [(i, i ^ bit) for i in range(ensembles)]
        everyone += [lax.ppermute(p, "member", pairs) for p in everyone]
        bit //= 2
    total = members * ensembles
    known = max(len(everyone) - 1, 1)
    base, factor = call(
        functools.partial(score_kernel, total),
        [
            jax.ShapeDtypeStruct((members, variables, points), F32),
            jax.ShapeDtypeStruct((variables, points), F32),
        ],
        [predicted, truth, area[None, :], var_weight[None, :], *everyone[1:known]],
        flops=8 * total * members * variables * points,
    )
    late_grad = jax.ShapeDtypeStruct(
        (members, groups, len(late) * capacity, per * points), BF16
    )
    *leaving_early, d_scores, d_attended = call(
        functools.partial(
            backward_kernel, members, total, len(early), capacity, head_size
        ),
        [chunk_shape] * len(early)
        + [late_grad, jax.ShapeDtypeStruct((members, per * points, width), BF16)],
        [
            query,
            w_key_t,
            w_value_t,
            w_out,
            predicted,
            base,
            factor,
            weights,
            values,
            *everyone[known:],
        ],
        scratch=[pltpu.VMEM((len(early) * step, width), BF16)] * 2
        + [
            pltpu.VMEM((len(early) * step, width), F32),
            pltpu.VMEM((members, width, per * points), BF16),
        ],
        flops=4 * members * received * width * width,
    )
    returned_early = exchanged(leaving_early, early, -1)
    leaving_late = call(
        functools.partial(late_rows_kernel, len(late), capacity, head_size),
        [chunk_shape] * len(late),
        [query, w_key_t, w_value_t, d_scores, weights, d_attended],
        scratch=[pltpu.VMEM((len(late) * step, width), BF16)] * 2,
        flops=4 * len(late) * step * width * width,
    )
    returned_late = exchanged(leaving_late, late, -1)
    before = call(
        functools.partial(first_sum_kernel, members, capacity),
        jax.ShapeDtypeStruct((members, own_rows, width), F32),
        [place_early, *returned_early],
        flops=2 * len(early) * step * own_rows * width,
    )
    return last_sum(members, capacity, place_late, before, returned_late)


def solution(mesh):
    return jax.shard_map(
        functools.partial(on_device, mesh.shape["grid"], mesh.shape["member"]),
        mesh=mesh,
        in_specs=(
            P("member", "grid", None),
            P("grid", None),
            P(),
            P(),
            P(),
            P(),
            P(None, "grid"),
            P("grid"),
            P(),
            P("grid", None, None),
            P("grid", None),
            P("grid"),
        ),
        out_specs=P("member", "grid", None),
        check_vma=False,
    )
```
